32 devices in a mesh: col: 4 (over y, core), row: 8 (over z, x).
Axes of the slice: x: 2, y: 2, z: 4, core: 2. Of those that a mesh axis runs over, the one named last changes fastest.
Arguments:
- panel: bfloat16 [8, 48, 512, 128], P('row', 'col'), may hold values from -6 to 6
- stiffness: bfloat16 [8, 48, 512, 512], P('row', 'col'), may hold values from -0.25 to 0.25
- mass: float32 [8, 48, 512], P('row', 'col'), may hold values from 0.2 to 2
- resident: bfloat16 [8, 24576, 1024], P('row', None, 'col'), may hold values from -0.01953125 to 0.01953125
- face_rows: int32 [8, 2, 2048], P('row'), may hold values from 0 to 24575, as said below
- counts: int32 [8], P('row'), may hold values from 24 to 48, as said below
Outputs:
- gram: float32 [1024, 128], P(('col', 'row'))
The draws below stay inside these ranges and needn't reach their ends.
Inputs may be any that keep to these rules, and one draw needn't show every extreme that they name: `counts`: each partition has between 24 and 48 live elements in its first slots; some partition has exactly 48. `face_rows`: each list of a partition holds 2048 distinct node rows of its live elements; its list 0 includes its last live node row.
All inputs are finite; a program needn't handle non-finite values.
Results may differ from the reference program's by a relative error of at most 0.0034.
Values may be sent and summed in bfloat16 or wider, within the bound.
A program may use at most 128 MiB of HBM per device.

```python
import math
import jax
import jax.numpy as jnp
from jax import lax

NODES = 512
SNAP = 128
RES = 1024
FACE_N = 2048
EL_CAP = 48
PARTITIONS = 8


def layout(key):
    base = jax.random.randint(jax.random.fold_in(key, 11), (PARTITIONS,), EL_CAP // 2, EL_CAP + 1)
    filled = jax.random.randint(jax.random.fold_in(key, 12), (), 0, PARTITIONS)
    counts = jnp.where(jnp.arange(PARTITIONS) == filled, EL_CAP, base).astype(jnp.int32)
    total_rows = EL_CAP * NODES
    position = jnp.arange(total_rows, dtype=jnp.int32)

    def lists(subkey, count):
        score = jax.random.randint(subkey, (2, total_rows), 0, 32768) * 32768 + position[None, :]
        last_live = (position[None, :] == count * NODES - 1) & (jnp.arange(2, dtype=jnp.int32)[:, None] == 0)
        score = jnp.where(last_live, -1, score)
        score = jnp.where(position[None, :] < count * NODES, score, score + 2 ** 30)
        order = jnp.argsort(score, axis=1, stable=True)
        return order[:, :FACE_N].astype(jnp.int32)
    subkeys = jax.random.split(jax.random.fold_in(key, 13), PARTITIONS)
    return (counts, jax.vmap(lists)(subkeys, counts))


def draw_counts(key, part):
    return layout(key)[0]


def draw_face_rows(key, part):
    return layout(key)[1]


def spiked(array, key, source, target, parts, factor):
    def block_of(dim):
        return (jnp.arange(array.shape[dim]) // (array.shape[dim] // parts)).reshape((-1,) + (1,) * (array.ndim - 1 - dim))

    near = jax.random.permutation(key, parts)[block_of(target)]
    far = (block_of(target) + parts // 2) % parts
    return jnp.where((block_of(source) == near) | (block_of(source) == far), factor * array, array)


def block_scale(own_key, dims, pieces, least, top_value):
    level = 1.0
    for dim, shards_of in pieces:
        draws = jax.random.uniform(jax.random.fold_in(jax.random.fold_in(own_key, 6), dim), (shards_of,), jnp.float32, least / len(pieces), top_value / len(pieces))
        level = level * jnp.repeat(jnp.exp(draws), dims[dim] // shards_of).reshape((-1,) + (1,) * (len(dims) - 1 - dim))
    return level


def gaussian(stream_key, shape, spread, limit, pieces=(), held_as=jnp.bfloat16):
    gain = block_scale(stream_key, shape, pieces, -0.22, 0.18) if pieces else 1.0
    drawn = jax.random.normal(stream_key, shape, jnp.float32) * spread * gain
    return jnp.minimum(jnp.maximum(drawn, -limit), limit).astype(held_as)


def heavy_noise(rng, shape, spread, limit, shards, heavy, kind=jnp.bfloat16):
    drawn = spread * jax.random.normal(rng, shape, jnp.float32)
    if shards:
        drawn = drawn * block_scale(rng, shape, shards, -0.22, 0.18)
    return jnp.clip(spiked(drawn, jax.random.fold_in(rng, 3), *heavy), -limit, limit).astype(kind)


def setup_inputs(seed: int = 0) -> dict:
    streams_of = jax.random.split(jax.random.key(seed), 7)
    panel = gaussian(streams_of[0], (PARTITIONS, EL_CAP, NODES, SNAP), 1.0, 6.0, ((0, 8), (1, 4)))
    stiffness = gaussian(streams_of[1], (PARTITIONS, EL_CAP, NODES, NODES), NODES ** -0.5, 0.25, ((0, 8), (1, 4)))
    mass = jnp.clip(jnp.exp(math.log(2.0) - 2.3025851 * jax.random.uniform(streams_of[2], (PARTITIONS, EL_CAP, NODES), jnp.float32) ** block_scale(streams_of[2], (PARTITIONS, EL_CAP, NODES), ((0, 8), (1, 4)), -0.2, 0.2)), 0.2, 2.0)
    resident = heavy_noise(streams_of[3], (PARTITIONS, EL_CAP * NODES, RES), (PARTITIONS * EL_CAP * NODES) ** -0.5, 0.01953125, ((0, 8), (2, 4)), (0, 2, 8, 2.0))
    face_rows = draw_face_rows(jax.random.fold_in(streams_of[6], 71), 0)
    counts = draw_counts(jax.random.fold_in(streams_of[6], 71), 0)
    return {"panel": panel, "stiffness": stiffness, "mass": mass, "resident": resident, "face_rows": face_rows, "counts": counts}


def apply_one(items):
    block, values, weights = items
    values = values.astype(jnp.float32)
    product = jnp.einsum("enm,ems->ens", block.astype(jnp.float32), values)
    return product + weights[:, :, None] * values


def add_faces(values, rows, from_next, from_prev):
    return values.at[rows[1]].add(from_next).at[rows[0]].add(from_prev)


def reference(panel, stiffness, mass, resident, face_rows, counts):
    applied = lax.map(apply_one, (stiffness, panel, mass))
    live = jnp.arange(EL_CAP, dtype=jnp.int32)[None, :] < counts[:, None]
    applied = jnp.where(live[:, :, None, None], applied, 0.0).astype(jnp.bfloat16)
    applied = applied.reshape(PARTITIONS, EL_CAP * NODES, SNAP)
    tiles = jax.vmap(lambda w, idx: w[idx])(applied, face_rows)
    blank = jnp.zeros((1, FACE_N, SNAP), jnp.bfloat16)
    from_next = jnp.concatenate([tiles[1:, 0], blank], axis=0).astype(jnp.float32)
    from_prev = jnp.concatenate([blank, tiles[:-1, 1]], axis=0).astype(jnp.float32)
    summed = jax.vmap(add_faces)(applied.astype(jnp.float32), face_rows, from_next, from_prev)
    summed = summed.astype(jnp.bfloat16)

    def step(total, items):
        left, right = items
        return total + jnp.dot(left.T, right, preferred_element_type=jnp.float32), None

    start = jnp.zeros((RES, SNAP), jnp.float32)
    gram, unused = lax.scan(step, start, (resident, summed))
    return gram
```

```python
import functools

import jax
import jax.numpy as jnp
from jax import lax
from jax.experimental import pallas as pl
from jax.experimental.pallas import tpu as pltpu
from jax.sharding import PartitionSpec as P

MESH = pl.DeviceIdType.MESH


def passed_along(value, axis, steps):
    count = lax.axis_size(axis)
    leading, last = (max(0, -steps), min(count, count - steps))
    return lax.ppermute(value, axis, [(source, source + steps) for source in range(leading, last)])


def scatter_sum_kernel(n, x_ref, out_ref, arrived, send_sem, recv_sem):
    me = lax.axis_index("row")
    column = lax.axis_index("col")
    own = out_ref.shape[0]
    barrier = pltpu.get_barrier_semaphore()
    for step in range(1, n):
        peer = lax.rem(me + step, n)
        pl.semaphore_signal(barrier, inc=1, device_id=(column, peer), device_id_type=MESH)
    pl.semaphore_wait(barrier, n - 1)
    copies = []
    for step in range(1, n):
        peer = lax.rem(me + step, n)
        copy = pltpu.make_async_remote_copy(
            src_ref=x_ref.at[pl.ds(pl.multiple_of(peer * own, own), own)],
            dst_ref=arrived.at[step - 1],
            send_sem=send_sem.at[step - 1],
            recv_sem=recv_sem.at[step - 1],
            device_id=(column, peer),
            device_id_type=MESH,
        )
        copy.start()
        copies.append(copy)
    total = x_ref[pl.ds(pl.multiple_of(me * own, own), own)]
    for step, copy in enumerate(copies):
        copy.wait()
        total = total + arrived[step]
    out_ref[...] = total


def scatter_sum(x):
    n = lax.axis_size("row")
    own = x.shape[0] // n
    return pl.pallas_call(
        functools.partial(scatter_sum_kernel, n),
        out_shape=jax.ShapeDtypeStruct((own, x.shape[1]), jnp.float32),
        in_specs=[pl.BlockSpec(memory_space=pltpu.VMEM)],
        out_specs=pl.BlockSpec(memory_space=pltpu.VMEM),
        scratch_shapes=[
            pltpu.VMEM((n - 1, own, x.shape[1]), jnp.float32),
            pltpu.SemaphoreType.DMA((n - 1,)),
            pltpu.SemaphoreType.DMA((n - 1,)),
        ],
        compiler_params=pltpu.CompilerParams(collective_id=0, has_side_effects=True),
    )(x)


def shards(panel, stiffness, mass, resident, face_rows, counts):
    slots = panel.shape[1]
    nodes = panel.shape[2]
    width = panel.shape[3]
    column = lax.axis_index("col")
    slot_ids = column * slots + jnp.arange(slots, dtype=jnp.int32)
    live = slot_ids < counts[0]
    values = panel[0]
    applied = jnp.einsum("enm,ems->ens", stiffness[0], values, preferred_element_type=jnp.float32)
    applied = applied + mass[0][:, :, None] * values.astype(jnp.float32)
    applied = jnp.where(live[:, None, None], applied, 0.0).astype(jnp.bfloat16)
    local_rows = applied.reshape(slots * nodes, width)
    whole = lax.all_gather(local_rows, "col", axis=0, tiled=True)
    prev_rows = face_rows[0, 0]
    next_rows = face_rows[0, 1]
    columns = resident[0]
    at_next = columns[next_rows]
    at_prev = columns[prev_rows]
    from_next = passed_along(whole[prev_rows], "row", -1)
    from_prev = passed_along(whole[next_rows], "row", 1)
    contract = (((0,), (0,)), ((), ()))
    partial_gram = lax.dot_general(columns, whole, contract, preferred_element_type=jnp.float32)
    partial_gram += lax.dot_general(at_next, from_next, contract, preferred_element_type=jnp.float32)
    partial_gram += lax.dot_general(at_prev, from_prev, contract, preferred_element_type=jnp.float32)
    return scatter_sum(partial_gram)


def solution(mesh):
    in_specs = (
        P("row", "col", None, None),
        P("row", "col", None, None),
        P("row", "col", None),
        P("row", None, "col"),
        P("row", None, None),
        P("row"),
    )
    out_specs = P(("col", "row"), None)
    return jax.shard_map(shards, mesh=mesh, in_specs=in_specs, out_specs=out_specs, check_vma=False)
```

```python
import functools

import jax
import jax.numpy as jnp
from jax import lax
from jax.experimental import pallas as pl
from jax.experimental.pallas import tpu as pltpu
from jax.sharding import PartitionSpec as P

MESH = pl.DeviceIdType.MESH
ROWS_FIRST = (((0,), (0,)), ((), ()))
DEPTH = 4
GATHER_PIECES = 8
GROUP = 8


def gram_kernel(
    n, panel, mass, counts, faces, stiffness, resident, out,
    applied, res, wide, kbuf, rbuf, res_rows, picked, leaving, arrived, acc, gram, terms,
    k_sem, r_sem, far_send, far_recv, mate_send, mate_recv, on_send, on_recv,
    face_send, face_recv, ffar_send, ffar_recv, fmate_send, fmate_recv, fon_send, fon_recv,
    sum_send, sum_recv,
):
    me = lax.axis_index("row")
    c = lax.axis_index("col")
    mate = (c // 2) * 2 + (1 - c % 2)
    far = (1 - c // 2) * 2 + c % 2
    opposite = (1 - c // 2) * 2 + (1 - c % 2)
    slots, nodes = panel.shape[1], panel.shape[2]
    face_n = faces.shape[2]
    quarter = face_n // 4
    own = out.shape[0]
    all_slots = applied.shape[0]

    def stiff_copy(e):
        return pltpu.make_async_copy(stiffness.at[0, e], kbuf.at[e % DEPTH], k_sem.at[e % DEPTH])

    def res_copy(s):
        rows = pl.ds(pl.multiple_of(s * nodes, nodes), nodes)
        return pltpu.make_async_copy(resident.at[0, rows], rbuf.at[s % DEPTH], r_sem.at[s % DEPTH])

    def to(buffer, index, send, recv, k, column):
        return pltpu.make_async_remote_copy(
            src_ref=buffer.at[index], dst_ref=buffer.at[index], send_sem=send.at[k], recv_sem=recv.at[k],
            device_id=(column, me), device_id_type=MESH)

    for e in range(DEPTH):
        stiff_copy(e).start()
    for s in range(DEPTH):
        res_copy(s).start()
    barrier = pltpu.get_barrier_semaphore()
    for step in range(1, n):
        pl.semaphore_signal(barrier, inc=1, device_id=(c, lax.rem(me + step, n)), device_id_type=MESH)
    for column in (mate, far):
        pl.semaphore_signal(barrier, inc=1, device_id=(column, me), device_id_type=MESH)
    pl.semaphore_wait(barrier, n + 1)

    acc[...] = jnp.zeros_like(acc)
    node_ids = lax.broadcasted_iota(jnp.int32, (nodes, mass.shape[1]), 1)

    def apply_slot(e, carry):
        stiff_copy(e).wait()
        values = panel[0, e]
        product = jnp.dot(kbuf[e % DEPTH], values, preferred_element_type=jnp.float32)
        weight = jnp.sum(jnp.where(node_ids == e, mass[...], 0.0), axis=1, keepdims=True)
        product = product + weight * values.astype(jnp.float32)
        live = jnp.where(c * slots + e < counts[0], 1.0, 0.0)
        applied[c * slots + e] = (product * live).astype(jnp.bfloat16)
        to(applied, c * slots + e, far_send, far_recv, e, far).start()
        to(applied, c * slots + e, mate_send, mate_recv, e, mate).start()

        @pl.when(e + DEPTH < slots)
        def _():
            stiff_copy(e + DEPTH).start()
        return carry

    lax.fori_loop(0, slots, apply_slot, 0)

    def widen_resident(s, carry):
        res_copy(s).wait()
        res[pl.ds(pl.multiple_of(s * nodes, nodes), nodes), :] = rbuf[s % DEPTH].astype(jnp.float32)

        @pl.when(s + DEPTH < all_slots)
        def _():
            res_copy(s + DEPTH).start()
        return carry

    lax.fori_loop(0, all_slots, widen_resident, 0)

    def add_slot(slot):
        rows = pl.ds(pl.multiple_of(slot * nodes, nodes), nodes)
        block = applied[slot]
        wide[rows, :] = block.astype(jnp.float32)
        acc[...] += lax.dot_general(
            block, res[rows, :].astype(jnp.bfloat16), ROWS_FIRST, preferred_element_type=jnp.float32)

    piece_groups = 2 * face_n // GROUP // GATHER_PIECES

    def gather_resident(piece):
        def group(i, carry):
            g = piece * piece_groups + i
            for t in range(GROUP):
                j = g * GROUP + t
                row = faces[0, j // face_n, j % face_n]
                res_rows[g, t:t + 1, :] = res[pl.ds(row, 1), :]
            return carry
        lax.fori_loop(0, piece_groups, group, 0)

    def exchange_slot(e, carry):
        add_slot(c * slots + e)
        to(applied, mate * slots + e, mate_send, mate_recv, e, mate).wait_recv()
        add_slot(mate * slots + e)

        @pl.when(e < GATHER_PIECES)
        def _():
            gather_resident(e)

        to(applied, far * slots + e, far_send, far_recv, e, far).wait_recv()
        to(applied, far * slots + e, on_send, on_recv, e, mate).start()
        add_slot(far * slots + e)

        @pl.when(e > 0)
        def _():
            to(applied, opposite * slots + e - 1, on_send, on_recv, e - 1, mate).wait_recv()
            add_slot(opposite * slots + e - 1)
        return carry

    lax.fori_loop(0, slots, exchange_slot, 0)
    to(applied, opposite * slots + slots - 1, on_send, on_recv, slots - 1, mate).wait_recv()
    add_slot(opposite * slots + slots - 1)

    has = (me < n - 1, me > 0)
    target = (jnp.maximum(me - 1, 0), jnp.minimum(me + 1, n - 1))
    sends = (me > 0, me < n - 1)

    def face_copy(l):
        return pltpu.make_async_remote_copy(
            src_ref=leaving.at[l], dst_ref=arrived.at[l, c], send_sem=face_send.at[l], recv_sem=face_recv.at[l],
            device_id=(c, target[l]), device_id_type=MESH)

    for l in range(2):
        def group(i, carry, l=l):
            for t in range(GROUP):
                row = faces[0, l, c * quarter + i * GROUP + t]
                picked[i, t:t + 1, :] = wide[pl.ds(row, 1), :]
            return carry
        lax.fori_loop(0, quarter // GROUP, group, 0)
        leaving[l] = picked[...].reshape(quarter, picked.shape[2]).astype(jnp.bfloat16)

        @pl.when(sends[l])
        def _(l=l):
            face_copy(l).start()

    def share(l, column, send, recv, to_column):
        return pltpu.make_async_remote_copy(
            src_ref=arrived.at[l, column], dst_ref=arrived.at[l, column], send_sem=send.at[l], recv_sem=recv.at[l],
            device_id=(to_column, me), device_id_type=MESH)

    def add_face(l, column):
        groups = quarter // GROUP
        start = (1 - l) * (face_n // GROUP) + column * groups
        rows = res_rows[pl.ds(start, groups)].reshape(quarter, res_rows.shape[2])
        acc[...] += lax.dot_general(
            arrived[l, column], rows.astype(jnp.bfloat16), ROWS_FIRST, preferred_element_type=jnp.float32)

    for l in range(2):
        @pl.when(has[l])
        def _(l=l):
            face_copy(l).wait_recv()

        @pl.when(jnp.logical_not(has[l]))
        def _(l=l):
            arrived[l, c] = jnp.zeros(arrived.shape[2:], jnp.bfloat16)

        share(l, c, ffar_send, ffar_recv, far).start()
        share(l, c, fmate_send, fmate_recv, mate).start()
    for l in range(2):
        add_face(l, c)
        share(l, mate, fmate_send, fmate_recv, mate).wait_recv()
        add_face(l, mate)
    for l in range(2):
        share(l, far, ffar_send, ffar_recv, far).wait_recv()
        share(l, far, fon_send, fon_recv, mate).start()
        add_face(l, far)
    for l in range(2):
        share(l, opposite, fon_send, fon_recv, mate).wait_recv()
        add_face(l, opposite)

    gram[...] = acc[...].T
    copies = []
    for step in range(1, n):
        peer = lax.rem(me + step, n)
        copy = pltpu.make_async_remote_copy(
            src_ref=gram.at[pl.ds(pl.multiple_of(peer * own, own), own)], dst_ref=terms.at[step - 1],
            send_sem=sum_send.at[step - 1], recv_sem=sum_recv.at[step - 1],
            device_id=(c, peer), device_id_type=MESH)
        copy.start()
        copies.append(copy)

    def drain(e, carry):
        to(applied, c * slots + e, far_send, far_recv, e, far).wait_send()
        to(applied, c * slots + e, mate_send, mate_recv, e, mate).wait_send()
        to(applied, far * slots + e, on_send, on_recv, e, mate).wait_send()
        return carry

    lax.fori_loop(0, slots, drain, 0)
    for l in range(2):
        @pl.when(sends[l])
        def _(l=l):
            face_copy(l).wait_send()
        share(l, c, ffar_send, ffar_recv, far).wait_send()
        share(l, c, fmate_send, fmate_recv, mate).wait_send()
        share(l, far, fon_send, fon_recv, mate).wait_send()
    total = gram[pl.ds(pl.multiple_of(me * own, own), own), :]
    for step, copy in enumerate(copies):
        copy.wait_recv()
        total = total + terms[step]
    for copy in copies:
        copy.wait_send()
    out[...] = total


def shards(panel, stiffness, mass, resident, face_rows, counts):
    n = lax.axis_size("row")
    columns = lax.axis_size("col")
    slots, nodes, width = panel.shape[1:]
    rows, kept = resident.shape[1:]
    face_n = face_rows.shape[2]
    quarter = face_n // columns
    own = kept // n
    bf16, f32 = jnp.bfloat16, jnp.float32
    dma = pltpu.SemaphoreType.DMA
    vmem = pl.BlockSpec(memory_space=pltpu.VMEM)
    smem = pl.BlockSpec(memory_space=pltpu.SMEM)
    anywhere = pl.BlockSpec(memory_space=pl.ANY)
    flops = 2 * slots * nodes * nodes * width + 2 * (rows + 2 * face_n) * kept * width
    return pl.pallas_call(
        functools.partial(gram_kernel, n),
        out_shape=jax.ShapeDtypeStruct((own, width), f32),
        in_specs=[vmem, vmem, smem, smem, anywhere, anywhere],
        out_specs=vmem,
        scratch_shapes=[
            pltpu.VMEM((columns * slots, nodes, width), bf16),
            pltpu.VMEM((rows, kept), f32),
            pltpu.VMEM((rows, width), f32),
            pltpu.VMEM((DEPTH, nodes, nodes), bf16),
            pltpu.VMEM((DEPTH, nodes, kept), bf16),
            pltpu.VMEM((2 * face_n // GROUP, GROUP, kept), f32),
            pltpu.VMEM((quarter // GROUP, GROUP, width), f32),
            pltpu.VMEM((2, quarter, width), bf16),
            pltpu.VMEM((2, columns, quarter, width), bf16),
            pltpu.VMEM((width, kept), f32),
            pltpu.VMEM((kept, width), f32),
            pltpu.VMEM((n - 1, own, width), f32),
            dma((DEPTH,)), dma((DEPTH,)),
            dma((slots,)), dma((slots,)), dma((slots,)), dma((slots,)), dma((slots,)), dma((slots,)),
            dma((2,)), dma((2,)), dma((2,)), dma((2,)), dma((2,)), dma((2,)), dma((2,)), dma((2,)),
            dma((n - 1,)), dma((n - 1,)),
        ],
        compiler_params=pltpu.CompilerParams(
            collective_id=0, has_side_effects=True, vmem_limit_bytes=62 * 1024 * 1024),
        cost_estimate=pl.CostEstimate(
            flops=flops, bytes_accessed=2 * (slots * nodes * (nodes + width) + rows * kept), transcendentals=0),
    )(panel, mass[0].T, counts, face_rows, stiffness, resident)


def solution(mesh):
    in_specs = (
        P("row", "col", None, None),
        P("row", "col", None, None),
        P("row", "col", None),
        P("row", None, "col"),
        P("row", None, None),
        P("row"),
    )
    out_specs = P(("col", "row"), None)
    return jax.shard_map(shards, mesh=mesh, in_specs=in_specs, out_specs=out_specs, check_vma=False)
```

```python
import functools

import jax
import jax.numpy as jnp
from jax import lax
from jax.experimental import pallas as pl
from jax.experimental.pallas import tpu as pltpu
from jax.sharding import PartitionSpec as P

MESH = pl.DeviceIdType.MESH
ROWS_FIRST = (((0,), (0,)), ((), ()))
DEPTH = 4
GATHER_PIECES = 8
GROUP = 8
BATCH = 16


def gram_kernel(
    n, panel, mass, counts, faces, stiffness, resident, out,
    applied, res, wide, kbuf, rbuf, res_rows, picked, leaving, arrived, acc, gram, terms,
    k_sem, r_sem, far_send, far_recv, mate_send, mate_recv, on_send, on_recv,
    face_send, face_recv, ffar_send, ffar_recv, fmate_send, fmate_recv, fon_send, fon_recv,
    sum_send, sum_recv,
):
    me = lax.axis_index("row")
    c = lax.axis_index("col")
    mate = (c // 2) * 2 + (1 - c % 2)
    far = (1 - c // 2) * 2 + c % 2
    opposite = (1 - c // 2) * 2 + (1 - c % 2)
    slots, nodes = panel.shape[1], panel.shape[2]
    face_n = faces.shape[2]
    quarter = face_n // 4
    own = out.shape[0]
    all_slots = applied.shape[0]

    def stiff_copy(e):
        return pltpu.make_async_copy(stiffness.at[0, e], kbuf.at[lax.rem(e, DEPTH)], k_sem.at[lax.rem(e, DEPTH)])

    def res_copy(s):
        rows = pl.ds(pl.multiple_of(s * nodes, nodes), nodes)
        return pltpu.make_async_copy(resident.at[0, rows], rbuf.at[lax.rem(s, DEPTH)], r_sem.at[lax.rem(s, DEPTH)])

    def to(buffer, index, send, recv, k, column):
        return pltpu.make_async_remote_copy(
            src_ref=buffer.at[index], dst_ref=buffer.at[index], send_sem=send.at[k], recv_sem=recv.at[k],
            device_id=(column, me), device_id_type=MESH)

    for e in range(DEPTH):
        stiff_copy(jnp.int32(e)).start()
    for s in range(DEPTH):
        res_copy(jnp.int32(s)).start()
    barrier = pltpu.get_barrier_semaphore()
    for step in range(1, n):
        pl.semaphore_signal(barrier, inc=1, device_id=(c, lax.rem(me + step, n)), device_id_type=MESH)
    for column in (mate, far):
        pl.semaphore_signal(barrier, inc=1, device_id=(column, me), device_id_type=MESH)
    pl.semaphore_wait(barrier, n + 1)

    acc[...] = jnp.zeros_like(acc)

    def node_weights(e):
        width = panel.shape[3]
        pieces = [jnp.broadcast_to(mass[e, :, k:k + width], (width, width)).T for k in range(0, nodes, width)]
        return jnp.concatenate(pieces, axis=0)

    def apply_slot(e, carry):
        stiff_copy(e).wait()
        values = panel[0, e]
        product = jnp.dot(kbuf[lax.rem(e, DEPTH)], values, preferred_element_type=jnp.float32)
        product = product + node_weights(e) * values.astype(jnp.float32)
        live = jnp.where(c * slots + e < counts[0], 1.0, 0.0)
        applied[c * slots + e] = (product * live).astype(jnp.bfloat16)
        to(applied, c * slots + e, far_send, far_recv, e, far).start()
        to(applied, c * slots + e, mate_send, mate_recv, e, mate).start()

        @pl.when(e + DEPTH < slots)
        def _():
            stiff_copy(e + DEPTH).start()
        return carry

    lax.fori_loop(0, slots, apply_slot, 0)

    def widen_resident(s, carry):
        res_copy(s).wait()
        res[pl.ds(pl.multiple_of(s * nodes, nodes), nodes), :] = rbuf[lax.rem(s, DEPTH)].astype(jnp.float32)

        @pl.when(s + DEPTH < all_slots)
        def _():
            res_copy(s + DEPTH).start()
        return carry

    lax.fori_loop(0, all_slots, widen_resident, 0)

    def add_slot(slot):
        rows = pl.ds(pl.multiple_of(slot * nodes, nodes), nodes)
        block = applied[slot]
        wide[rows, :] = block.astype(jnp.float32)
        acc[...] += lax.dot_general(
            block, res[rows, :].astype(jnp.bfloat16), ROWS_FIRST, preferred_element_type=jnp.float32)

    def gather_rows(source, l, first, target, target_first, count):
        def groups(i, carry):
            base = pl.multiple_of(first + i * BATCH, BATCH)
            rows = [faces[0, l, base + t] for t in range(BATCH)]
            values = [source[pl.ds(row, 1), :] for row in rows]
            for t, value in enumerate(values):
                target[target_first + i * (BATCH // GROUP) + t // GROUP, t % GROUP:t % GROUP + 1, :] = value
            return carry
        lax.fori_loop(0, count // BATCH, groups, 0)

    piece_rows = 2 * face_n // GATHER_PIECES
    half = GATHER_PIECES // 2

    def gather_resident(piece):
        gather_rows(res, lax.div(piece, half), lax.rem(piece, half) * piece_rows,
                    res_rows, piece * (piece_rows // GROUP), piece_rows)

    def exchange_slot(e, carry):
        add_slot(c * slots + e)
        to(applied, mate * slots + e, mate_send, mate_recv, e, mate).wait_recv()
        add_slot(mate * slots + e)

        @pl.when(e < GATHER_PIECES)
        def _():
            gather_resident(e)

        to(applied, far * slots + e, far_send, far_recv, e, far).wait_recv()
        to(applied, far * slots + e, on_send, on_recv, e, mate).start()
        add_slot(far * slots + e)

        @pl.when(e > 0)
        def _():
            to(applied, opposite * slots + e - 1, on_send, on_recv, e - 1, mate).wait_recv()
            add_slot(opposite * slots + e - 1)
        return carry

    lax.fori_loop(0, slots, exchange_slot, 0)
    to(applied, opposite * slots + slots - 1, on_send, on_recv, slots - 1, mate).wait_recv()
    add_slot(opposite * slots + slots - 1)

    has = (me < n - 1, me > 0)
    target = (jnp.maximum(me - 1, 0), jnp.minimum(me + 1, n - 1))
    sends = (me > 0, me < n - 1)

    def face_copy(l):
        return pltpu.make_async_remote_copy(
            src_ref=leaving.at[l], dst_ref=arrived.at[l, c], send_sem=face_send.at[l], recv_sem=face_recv.at[l],
            device_id=(c, target[l]), device_id_type=MESH)

    for l in range(2):
        gather_rows(wide, l, c * quarter, picked, 0, quarter)
        leaving[l] = picked[...].reshape(quarter, picked.shape[2]).astype(jnp.bfloat16)

        @pl.when(sends[l])
        def _(l=l):
            face_copy(l).start()

    def share(l, column, send, recv, to_column):
        return pltpu.make_async_remote_copy(
            src_ref=arrived.at[l, column], dst_ref=arrived.at[l, column], send_sem=send.at[l], recv_sem=recv.at[l],
            device_id=(to_column, me), device_id_type=MESH)

    def add_face(l, column):
        groups = quarter // GROUP
        start = (1 - l) * (face_n // GROUP) + column * groups
        rows = res_rows[pl.ds(start, groups)].reshape(quarter, res_rows.shape[2])
        acc[...] += lax.dot_general(
            arrived[l, column], rows.astype(jnp.bfloat16), ROWS_FIRST, preferred_element_type=jnp.float32)

    for l in range(2):
        @pl.when(has[l])
        def _(l=l):
            face_copy(l).wait_recv()

        @pl.when(jnp.logical_not(has[l]))
        def _(l=l):
            arrived[l, c] = jnp.zeros(arrived.shape[2:], jnp.bfloat16)

        share(l, c, ffar_send, ffar_recv, far).start()
        share(l, c, fmate_send, fmate_recv, mate).start()
    for l in range(2):
        add_face(l, c)
        share(l, mate, fmate_send, fmate_recv, mate).wait_recv()
        add_face(l, mate)
    for l in range(2):
        share(l, far, ffar_send, ffar_recv, far).wait_recv()
        share(l, far, fon_send, fon_recv, mate).start()
        add_face(l, far)
    for l in range(2):
        share(l, opposite, fon_send, fon_recv, mate).wait_recv()
        add_face(l, opposite)

    gram[...] = acc[...].T
    copies = []
    for step in range(1, n):
        peer = lax.rem(me + step, n)
        copy = pltpu.make_async_remote_copy(
            src_ref=gram.at[pl.ds(pl.multiple_of(peer * own, own), own)], dst_ref=terms.at[step - 1],
            send_sem=sum_send.at[step - 1], recv_sem=sum_recv.at[step - 1],
            device_id=(c, peer), device_id_type=MESH)
        copy.start()
        copies.append(copy)

    def drain(e, carry):
        to(applied, c * slots + e, far_send, far_recv, e, far).wait_send()
        to(applied, c * slots + e, mate_send, mate_recv, e, mate).wait_send()
        to(applied, far * slots + e, on_send, on_recv, e, mate).wait_send()
        return carry

    lax.fori_loop(0, slots, drain, 0)
    for l in range(2):
        @pl.when(sends[l])
        def _(l=l):
            face_copy(l).wait_send()
        share(l, c, ffar_send, ffar_recv, far).wait_send()
        share(l, c, fmate_send, fmate_recv, mate).wait_send()
        share(l, far, fon_send, fon_recv, mate).wait_send()
    total = gram[pl.ds(pl.multiple_of(me * own, own), own), :]
    for step, copy in enumerate(copies):
        copy.wait_recv()
        total = total + terms[step]
    for copy in copies:
        copy.wait_send()
    out[...] = total


def shards(panel, stiffness, mass, resident, face_rows, counts):
    n = lax.axis_size("row")
    columns = lax.axis_size("col")
    slots, nodes, width = panel.shape[1:]
    rows, kept = resident.shape[1:]
    face_n = face_rows.shape[2]
    quarter = face_n // columns
    own = kept // n
    bf16, f32 = jnp.bfloat16, jnp.float32
    dma = pltpu.SemaphoreType.DMA
    vmem = pl.BlockSpec(memory_space=pltpu.VMEM)
    smem = pl.BlockSpec(memory_space=pltpu.SMEM)
    anywhere = pl.BlockSpec(memory_space=pl.ANY)
    flops = 2 * slots * nodes * nodes * width + 2 * (rows + 2 * face_n) * kept * width
    return pl.pallas_call(
        functools.partial(gram_kernel, n),
        out_shape=jax.ShapeDtypeStruct((own, width), f32),
        in_specs=[vmem, vmem, smem, smem, anywhere, anywhere],
        out_specs=vmem,
        scratch_shapes=[
            pltpu.VMEM((columns * slots, nodes, width), bf16),
            pltpu.VMEM((rows, kept), f32),
            pltpu.VMEM((rows, width), f32),
            pltpu.VMEM((DEPTH, nodes, nodes), bf16),
            pltpu.VMEM((DEPTH, nodes, kept), bf16),
            pltpu.VMEM((2 * face_n // GROUP, GROUP, kept), f32),
            pltpu.VMEM((quarter // GROUP, GROUP, width), f32),
            pltpu.VMEM((2, quarter, width), bf16),
            pltpu.VMEM((2, columns, quarter, width), bf16),
            pltpu.VMEM((width, kept), f32),
            pltpu.VMEM((kept, width), f32),
            pltpu.VMEM((n - 1, own, width), f32),
            dma((DEPTH,)), dma((DEPTH,)),
            dma((slots,)), dma((slots,)), dma((slots,)), dma((slots,)), dma((slots,)), dma((slots,)),
            dma((2,)), dma((2,)), dma((2,)), dma((2,)), dma((2,)), dma((2,)), dma((2,)), dma((2,)),
            dma((n - 1,)), dma((n - 1,)),
        ],
        compiler_params=pltpu.CompilerParams(
            collective_id=0, has_side_effects=True, vmem_limit_bytes=62 * 1024 * 1024),
        cost_estimate=pl.CostEstimate(
            flops=flops, bytes_accessed=2 * (slots * nodes * (nodes + width) + rows * kept), transcendentals=0),
    )(panel, mass.transpose(1, 0, 2), counts, face_rows, stiffness, resident)


def solution(mesh):
    in_specs = (
        P("row", "col", None, None),
        P("row", "col", None, None),
        P("row", "col", None),
        P("row", None, "col"),
        P("row", None, None),
        P("row"),
    )
    out_specs = P(("col", "row"), None)
    return jax.shard_map(shards, mesh=mesh, in_specs=in_specs, out_specs=out_specs, check_vma=False)
```

```python
import functools

import jax
import jax.numpy as jnp
from jax import lax
from jax.experimental import pallas as pl
from jax.experimental.pallas import tpu as pltpu
from jax.sharding import PartitionSpec as P

MESH = pl.DeviceIdType.MESH
ROWS_FIRST = (((0,), (0,)), ((), ()))
DEPTH = 4
RES_DEPTH = 16
GATHER_PIECES = 8
GROUP = 8
BATCH = 16


def gram_kernel(
    n, panel, mass, counts, faces, stiffness, resident, out,
    applied, res, wide, kbuf, pbuf, rbuf, res_rows, picked, leaving, arrived, acc, gram, terms,
    k_sem, p_sem, r_sem, far_send, far_recv, mate_send, mate_recv, on_send, on_recv,
    face_send, face_recv, ffar_send, ffar_recv, fmate_send, fmate_recv, fon_send, fon_recv,
    sum_send, sum_recv,
):
    me = lax.axis_index("row")
    c = lax.axis_index("col")
    mate = (c // 2) * 2 + (1 - c % 2)
    far = (1 - c // 2) * 2 + c % 2
    opposite = (1 - c // 2) * 2 + (1 - c % 2)
    slots, nodes = panel.shape[1], panel.shape[2]
    face_n = faces.shape[2]
    quarter = face_n // 4
    own = out.shape[0]
    all_slots = applied.shape[0]

    def stiff_copy(e):
        return pltpu.make_async_copy(stiffness.at[0, e], kbuf.at[lax.rem(e, DEPTH)], k_sem.at[lax.rem(e, DEPTH)])

    def res_copy(s):
        rows = pl.ds(pl.multiple_of(s * nodes, nodes), nodes)
        return pltpu.make_async_copy(resident.at[0, rows], rbuf.at[lax.rem(s, RES_DEPTH)], r_sem.at[lax.rem(s, RES_DEPTH)])

    def panel_copy(e):
        return pltpu.make_async_copy(panel.at[0, e], pbuf.at[e], p_sem.at[e])

    def to(buffer, index, send, recv, k, column):
        return pltpu.make_async_remote_copy(
            src_ref=buffer.at[index], dst_ref=buffer.at[index], send_sem=send.at[k], recv_sem=recv.at[k],
            device_id=(column, me), device_id_type=MESH)

    for e in range(slots):
        if e < DEPTH:
            stiff_copy(jnp.int32(e)).start()
        panel_copy(e).start()
    for s in range(RES_DEPTH):
        res_copy(jnp.int32(s)).start()
    barrier = pltpu.get_barrier_semaphore()
    for step in range(1, n):
        pl.semaphore_signal(barrier, inc=1, device_id=(c, lax.rem(me + step, n)), device_id_type=MESH)
    for column in (mate, far):
        pl.semaphore_signal(barrier, inc=1, device_id=(column, me), device_id_type=MESH)
    pl.semaphore_wait(barrier, n + 1)

    acc[...] = jnp.zeros_like(acc)

    def node_weights(e):
        width = panel.shape[3]
        pieces = [jnp.broadcast_to(mass[e, :, k:k + width], (width, width)).T for k in range(0, nodes, width)]
        return jnp.concatenate(pieces, axis=0)

    def apply_slot(e, carry):
        stiff_copy(e).wait()
        panel_copy(e).wait()
        values = pbuf[e]
        product = jnp.dot(kbuf[lax.rem(e, DEPTH)], values, preferred_element_type=jnp.float32)
        product = product + node_weights(e) * values.astype(jnp.float32)
        live = jnp.where(c * slots + e < counts[0], 1.0, 0.0)
        applied[c * slots + e] = (product * live).astype(jnp.bfloat16)
        to(applied, c * slots + e, far_send, far_recv, e, far).start()
        to(applied, c * slots + e, mate_send, mate_recv, e, mate).start()

        @pl.when(e + DEPTH < slots)
        def _():
            stiff_copy(e + DEPTH).start()
        return carry

    lax.fori_loop(0, slots, apply_slot, 0)

    def widen_resident(s, carry):
        res_copy(s).wait()
        res[pl.ds(pl.multiple_of(s * nodes, nodes), nodes), :] = rbuf[lax.rem(s, RES_DEPTH)].astype(jnp.float32)

        @pl.when(s + RES_DEPTH < all_slots)
        def _():
            res_copy(s + RES_DEPTH).start()
        return carry

    lax.fori_loop(0, all_slots, widen_resident, 0)

    def add_slots(*which):
        total = None
        for slot in which:
            rows = pl.ds(pl.multiple_of(slot * nodes, nodes), nodes)
            block = applied[slot]
            wide[rows, :] = block.astype(jnp.float32)
            term = lax.dot_general(
                block, res[rows, :].astype(jnp.bfloat16), ROWS_FIRST, preferred_element_type=jnp.float32)
            total = term if total is None else total + term
        acc[...] += total

    def gather_rows(source, l, first, target, target_first, count):
        def groups(i, carry):
            base = pl.multiple_of(first + i * BATCH, BATCH)
            rows = [faces[0, l, base + t] for t in range(BATCH)]
            values = [source[pl.ds(row, 1), :] for row in rows]
            for t, value in enumerate(values):
                target[target_first + i * (BATCH // GROUP) + t // GROUP, t % GROUP:t % GROUP + 1, :] = value
            return carry
        lax.fori_loop(0, count // BATCH, groups, 0)

    piece_rows = 2 * face_n // GATHER_PIECES
    half = GATHER_PIECES // 2

    def gather_resident(piece):
        gather_rows(res, lax.div(piece, half), lax.rem(piece, half) * piece_rows,
                    res_rows, piece * (piece_rows // GROUP), piece_rows)

    def near_slots(e):
        to(applied, mate * slots + e, mate_send, mate_recv, e, mate).wait_recv()
        add_slots(c * slots + e, mate * slots + e)

        @pl.when(e < GATHER_PIECES)
        def _():
            gather_resident(e)

        to(applied, far * slots + e, far_send, far_recv, e, far).wait_recv()
        to(applied, far * slots + e, on_send, on_recv, e, mate).start()

    def exchange_slot(e, carry):
        near_slots(e)
        to(applied, opposite * slots + e - 1, on_send, on_recv, e - 1, mate).wait_recv()
        add_slots(far * slots + e, opposite * slots + e - 1)
        return carry

    near_slots(jnp.int32(0))
    add_slots(far * slots)
    lax.fori_loop(1, slots, exchange_slot, 0)
    to(applied, opposite * slots + slots - 1, on_send, on_recv, slots - 1, mate).wait_recv()
    add_slots(opposite * slots + slots - 1)

    has = (me < n - 1, me > 0)
    target = (jnp.maximum(me - 1, 0), jnp.minimum(me + 1, n - 1))
    sends = (me > 0, me < n - 1)

    def face_copy(l):
        return pltpu.make_async_remote_copy(
            src_ref=leaving.at[l], dst_ref=arrived.at[l, c], send_sem=face_send.at[l], recv_sem=face_recv.at[l],
            device_id=(c, target[l]), device_id_type=MESH)

    for l in range(2):
        gather_rows(wide, l, c * quarter, picked, 0, quarter)
        leaving[l] = picked[...].reshape(quarter, picked.shape[2]).astype(jnp.bfloat16)

        @pl.when(sends[l])
        def _(l=l):
            face_copy(l).start()

    def share(l, column, send, recv, to_column):
        return pltpu.make_async_remote_copy(
            src_ref=arrived.at[l, column], dst_ref=arrived.at[l, column], send_sem=send.at[l], recv_sem=recv.at[l],
            device_id=(to_column, me), device_id_type=MESH)

    def add_face(l, column):
        groups = quarter // GROUP
        start = (1 - l) * (face_n // GROUP) + column * groups
        rows = res_rows[pl.ds(start, groups)].reshape(quarter, res_rows.shape[2])
        acc[...] += lax.dot_general(
            arrived[l, column], rows.astype(jnp.bfloat16), ROWS_FIRST, preferred_element_type=jnp.float32)

    for l in range(2):
        @pl.when(has[l])
        def _(l=l):
            face_copy(l).wait_recv()

        @pl.when(jnp.logical_not(has[l]))
        def _(l=l):
            arrived[l, c] = jnp.zeros(arrived.shape[2:], jnp.bfloat16)

        share(l, c, ffar_send, ffar_recv, far).start()
        share(l, c, fmate_send, fmate_recv, mate).start()
    for l in range(2):
        add_face(l, c)
        share(l, mate, fmate_send, fmate_recv, mate).wait_recv()
        add_face(l, mate)
    for l in range(2):
        share(l, far, ffar_send, ffar_recv, far).wait_recv()
        share(l, far, fon_send, fon_recv, mate).start()
        add_face(l, far)
    for l in range(2):
        share(l, opposite, fon_send, fon_recv, mate).wait_recv()
        add_face(l, opposite)

    gram[...] = acc[...].T
    copies = []
    for step in range(1, n):
        peer = lax.rem(me + step, n)
        copy = pltpu.make_async_remote_copy(
            src_ref=gram.at[pl.ds(pl.multiple_of(peer * own, own), own)], dst_ref=terms.at[step - 1],
            send_sem=sum_send.at[step - 1], recv_sem=sum_recv.at[step - 1],
            device_id=(c, peer), device_id_type=MESH)
        copy.start()
        copies.append(copy)

    def drain(e, carry):
        to(applied, c * slots + e, far_send, far_recv, e, far).wait_send()
        to(applied, c * slots + e, mate_send, mate_recv, e, mate).wait_send()
        to(applied, far * slots + e, on_send, on_recv, e, mate).wait_send()
        return carry

    lax.fori_loop(0, slots, drain, 0)
    for l in range(2):
        @pl.when(sends[l])
        def _(l=l):
            face_copy(l).wait_send()
        share(l, c, ffar_send, ffar_recv, far).wait_send()
        share(l, c, fmate_send, fmate_recv, mate).wait_send()
        share(l, far, fon_send, fon_recv, mate).wait_send()
    total = gram[pl.ds(pl.multiple_of(me * own, own), own), :]
    for step, copy in enumerate(copies):
        copy.wait_recv()
        total = total + terms[step]
    for copy in copies:
        copy.wait_send()
    out[...] = total


def shards(panel, stiffness, mass, resident, face_rows, counts):
    n = lax.axis_size("row")
    columns = lax.axis_size("col")
    slots, nodes, width = panel.shape[1:]
    rows, kept = resident.shape[1:]
    face_n = face_rows.shape[2]
    quarter = face_n // columns
    own = kept // n
    bf16, f32 = jnp.bfloat16, jnp.float32
    dma = pltpu.SemaphoreType.DMA
    vmem = pl.BlockSpec(memory_space=pltpu.VMEM)
    smem = pl.BlockSpec(memory_space=pltpu.SMEM)
    anywhere = pl.BlockSpec(memory_space=pl.ANY)
    flops = 2 * slots * nodes * nodes * width + 2 * (rows + 2 * face_n) * kept * width
    return pl.pallas_call(
        functools.partial(gram_kernel, n),
        out_shape=jax.ShapeDtypeStruct((own, width), f32),
        in_specs=[anywhere, vmem, smem, smem, anywhere, anywhere],
        out_specs=vmem,
        scratch_shapes=[
            pltpu.VMEM((columns * slots, nodes, width), bf16),
            pltpu.VMEM((rows, kept), f32),
            pltpu.VMEM((rows, width), f32),
            pltpu.VMEM((DEPTH, nodes, nodes), bf16),
            pltpu.VMEM((slots, nodes, width), bf16),
            pltpu.VMEM((RES_DEPTH, nodes, kept), bf16),
            pltpu.VMEM((2 * face_n // GROUP, GROUP, kept), f32),
            pltpu.VMEM((quarter // GROUP, GROUP, width), f32),
            pltpu.VMEM((2, quarter, width), bf16),
            pltpu.VMEM((2, columns, quarter, width), bf16),
            pltpu.VMEM((width, kept), f32),
            pltpu.VMEM((kept, width), f32),
            pltpu.VMEM((n - 1, own, width), f32),
            dma((DEPTH,)), dma((slots,)), dma((RES_DEPTH,)),
            dma((slots,)), dma((slots,)), dma((slots,)), dma((slots,)), dma((slots,)), dma((slots,)),
            dma((2,)), dma((2,)), dma((2,)), dma((2,)), dma((2,)), dma((2,)), dma((2,)), dma((2,)),
            dma((n - 1,)), dma((n - 1,)),
        ],
        compiler_params=pltpu.CompilerParams(
            collective_id=0, has_side_effects=True, vmem_limit_bytes=62 * 1024 * 1024),
        cost_estimate=pl.CostEstimate(
            flops=flops, bytes_accessed=2 * (slots * nodes * (nodes + width) + rows * kept), transcendentals=0),
    )(panel, mass.transpose(1, 0, 2), counts, face_rows, stiffness, resident)


def solution(mesh):
    in_specs = (
        P("row", "col", None, None),
        P("row", "col", None, None),
        P("row", "col", None),
        P("row", None, "col"),
        P("row", None, None),
        P("row"),
    )
    out_specs = P(("col", "row"), None)
    return jax.shard_map(shards, mesh=mesh, in_specs=in_specs, out_specs=out_specs, check_vma=False)
```

```python
import functools

import jax
import jax.numpy as jnp
from jax import lax
from jax.experimental import pallas as pl
from jax.experimental.pallas import tpu as pltpu
from jax.sharding import PartitionSpec as P

MESH = pl.DeviceIdType.MESH
ROWS_FIRST = (((0,), (0,)), ((), ()))
DEPTH = 4
RES_DEPTH = 16
PIECES = 4
GROUP = 8


def gram_kernel(
    n, panel, mass, counts, faces, stiffness, resident, out,
    applied, res, wide, kbuf, pbuf, rbuf, res_picked, res_rows, other_rows, picked, half_picked, leaving, arrived, acc, gram, terms,
    k_sem, p_sem, r_sem, far_send, far_recv, mate_send, mate_recv, on_send, on_recv,
    face_send, face_recv, ffar_send, ffar_recv, fmate_send, fmate_recv, fon_send, fon_recv,
    row_send, row_recv, sum_send, sum_recv,
):
    me = lax.axis_index("row")
    c = lax.axis_index("col")
    mate = (c // 2) * 2 + (1 - c % 2)
    far = (1 - c // 2) * 2 + c % 2
    opposite = (1 - c // 2) * 2 + (1 - c % 2)
    slots, nodes = panel.shape[1], panel.shape[2]
    face_n = faces.shape[2]
    quarter = face_n // PIECES
    half = quarter // 2
    following = jnp.minimum(me + 1, n - 1)
    own = out.shape[0]
    all_slots = applied.shape[0]

    def stiff_copy(e):
        return pltpu.make_async_copy(stiffness.at[0, e], kbuf.at[lax.rem(e, DEPTH)], k_sem.at[lax.rem(e, DEPTH)])

    def res_copy(s):
        rows = pl.ds(pl.multiple_of(s * nodes, nodes), nodes)
        return pltpu.make_async_copy(resident.at[0, rows], rbuf.at[lax.rem(s, RES_DEPTH)], r_sem.at[lax.rem(s, RES_DEPTH)])

    def panel_copy(e):
        return pltpu.make_async_copy(panel.at[0, e], pbuf.at[e], p_sem.at[e])

    def to(buffer, index, send, recv, k, column):
        return pltpu.make_async_remote_copy(
            src_ref=buffer.at[index], dst_ref=buffer.at[index], send_sem=send.at[k], recv_sem=recv.at[k],
            device_id=(column, me), device_id_type=MESH)

    for e in range(slots):
        if e < DEPTH:
            stiff_copy(jnp.int32(e)).start()
        panel_copy(e).start()
    for s in range(RES_DEPTH):
        res_copy(jnp.int32(s)).start()
    barrier = pltpu.get_barrier_semaphore()
    for step in range(1, n):
        pl.semaphore_signal(barrier, inc=1, device_id=(c, lax.rem(me + step, n)), device_id_type=MESH)
    for column in (mate, far):
        pl.semaphore_signal(barrier, inc=1, device_id=(column, me), device_id_type=MESH)
    pl.semaphore_wait(barrier, n + 1)

    acc[...] = jnp.zeros_like(acc)

    def node_weights(e):
        width = panel.shape[3]
        pieces = [jnp.broadcast_to(mass[e, :, k:k + width], (width, width)).T for k in range(0, nodes, width)]
        return jnp.concatenate(pieces, axis=0)

    def widen_resident(s):
        res_copy(s).wait()
        res[pl.ds(pl.multiple_of(s * nodes, nodes), nodes), :] = rbuf[lax.rem(s, RES_DEPTH)].astype(jnp.float32)

        @pl.when(s + RES_DEPTH < all_slots)
        def _():
            res_copy(s + RES_DEPTH).start()

    def apply_slot(e, carry):
        stiff_copy(e).wait()
        panel_copy(e).wait()
        values = pbuf[e]
        product = jnp.dot(kbuf[lax.rem(e, DEPTH)], values, preferred_element_type=jnp.float32)
        product = product + node_weights(e) * values.astype(jnp.float32)
        live = jnp.where(c * slots + e < counts[0], 1.0, 0.0)
        applied[c * slots + e] = (product * live).astype(jnp.bfloat16)
        to(applied, c * slots + e, far_send, far_recv, e, far).start()
        to(applied, c * slots + e, mate_send, mate_recv, e, mate).start()

        @pl.when(e + DEPTH < slots)
        def _():
            stiff_copy(e + DEPTH).start()

        for t in range(all_slots // slots):
            widen_resident(e * (all_slots // slots) + t)
        return carry

    lax.fori_loop(0, slots, apply_slot, 0)

    def add_slots(*which):
        total = None
        for slot in which:
            rows = pl.ds(pl.multiple_of(slot * nodes, nodes), nodes)
            block = applied[slot]
            wide[rows, :] = block.astype(jnp.float32)
            term = lax.dot_general(
                block, res[rows, :].astype(jnp.bfloat16), ROWS_FIRST, preferred_element_type=jnp.float32)
            total = term if total is None else total + term
        acc[...] += total

    def gather_rows(source, l, first, target, count, batch):
        def groups(i, carry):
            base = pl.multiple_of(first + i * batch, batch)
            rows = [faces[0, l, base + t] for t in range(batch)]
            values = [source[pl.ds(row, 1), :] for row in rows]
            for t, value in enumerate(values):
                target[i * (batch // GROUP) + t // GROUP, t % GROUP:t % GROUP + 1, :] = value
            return carry
        lax.fori_loop(0, count // batch, groups, 0)

    def row_copy(piece):
        return pltpu.make_async_remote_copy(
            src_ref=res_rows.at[piece], dst_ref=other_rows.at[piece],
            send_sem=row_send.at[piece], recv_sem=row_recv.at[piece],
            device_id=(c, following), device_id_type=MESH)

    def gather_resident(piece):
        gather_rows(res, 1 - lax.div(piece, PIECES), lax.rem(piece, PIECES) * quarter, res_picked, quarter, 16)
        res_rows[piece] = res_picked[...].reshape(quarter, res_picked.shape[2]).astype(jnp.bfloat16)

        @pl.when(jnp.logical_and(piece < PIECES, me < n - 1))
        def _():
            row_copy(piece).start()

    def near_slots(e):
        to(applied, mate * slots + e, mate_send, mate_recv, e, mate).wait_recv()
        add_slots(c * slots + e, mate * slots + e)

        @pl.when(e < 2 * PIECES)
        def _():
            gather_resident(e)

        to(applied, far * slots + e, far_send, far_recv, e, far).wait_recv()
        to(applied, far * slots + e, on_send, on_recv, e, mate).start()

    def exchange_slot(e, carry):
        near_slots(e)
        to(applied, opposite * slots + e - 1, on_send, on_recv, e - 1, mate).wait_recv()
        add_slots(far * slots + e, opposite * slots + e - 1)
        return carry

    near_slots(jnp.int32(0))
    add_slots(far * slots)
    lax.fori_loop(1, slots, exchange_slot, 0)
    to(applied, opposite * slots + slots - 1, on_send, on_recv, slots - 1, mate).wait_recv()
    add_slots(opposite * slots + slots - 1)

    def face_copy(h):
        return pltpu.make_async_remote_copy(
            src_ref=leaving.at[h], dst_ref=arrived.at[h, c], send_sem=face_send.at[h], recv_sem=face_recv.at[h],
            device_id=(c, following), device_id_type=MESH)

    def share(h, column, send, recv, to_column):
        return pltpu.make_async_remote_copy(
            src_ref=arrived.at[h, column], dst_ref=arrived.at[h, column], send_sem=send.at[h], recv_sem=recv.at[h],
            device_id=(to_column, me), device_id_type=MESH)

    def add_face(h, column):
        acc[...] += lax.dot_general(
            arrived[h, column], res_rows[PIECES + column, h * half:(h + 1) * half], ROWS_FIRST,
            preferred_element_type=jnp.float32)

    def add_other(piece):
        gather_rows(wide, 0, piece * quarter, picked, quarter, 32)
        row_copy(jnp.int32(piece)).wait_recv()
        block = picked[...].reshape(quarter, picked.shape[2]).astype(jnp.bfloat16)
        acc[...] += lax.dot_general(block, other_rows[piece], ROWS_FIRST, preferred_element_type=jnp.float32)

    @pl.when(me < n - 1)
    def _():
        for h in range(2):
            gather_rows(wide, 1, c * quarter + h * half, half_picked, half, 32)
            leaving[h] = half_picked[...].reshape(half, half_picked.shape[2]).astype(jnp.bfloat16)
            face_copy(h).start()

    @pl.when(me > 0)
    def _():
        for h in range(2):
            add_other(h)
            face_copy(h).wait_recv()
            share(h, c, ffar_send, ffar_recv, far).start()
            share(h, c, fmate_send, fmate_recv, mate).start()
        for h in range(2):
            add_other(2 + h)
            share(h, far, ffar_send, ffar_recv, far).wait_recv()
            share(h, far, fon_send, fon_recv, mate).start()
        for h in range(2):
            add_face(h, c)
            add_face(h, far)
            share(h, mate, fmate_send, fmate_recv, mate).wait_recv()
            add_face(h, mate)
        for h in range(2):
            share(h, opposite, fon_send, fon_recv, mate).wait_recv()
            add_face(h, opposite)

    gram[...] = acc[...].T
    copies = []
    for step in range(1, n):
        peer = lax.rem(me + step, n)
        copy = pltpu.make_async_remote_copy(
            src_ref=gram.at[pl.ds(pl.multiple_of(peer * own, own), own)], dst_ref=terms.at[step - 1],
            send_sem=sum_send.at[step - 1], recv_sem=sum_recv.at[step - 1],
            device_id=(c, peer), device_id_type=MESH)
        copy.start()
        copies.append(copy)

    def drain(e, carry):
        to(applied, c * slots + e, far_send, far_recv, e, far).wait_send()
        to(applied, c * slots + e, mate_send, mate_recv, e, mate).wait_send()
        to(applied, far * slots + e, on_send, on_recv, e, mate).wait_send()
        return carry

    lax.fori_loop(0, slots, drain, 0)

    @pl.when(me < n - 1)
    def _():
        for h in range(2):
            face_copy(h).wait_send()
        for piece in range(PIECES):
            row_copy(jnp.int32(piece)).wait_send()

    @pl.when(me > 0)
    def _():
        for h in range(2):
            share(h, c, ffar_send, ffar_recv, far).wait_send()
            share(h, c, fmate_send, fmate_recv, mate).wait_send()
            share(h, far, fon_send, fon_recv, mate).wait_send()

    total = gram[pl.ds(pl.multiple_of(me * own, own), own), :]
    for step, copy in enumerate(copies):
        copy.wait_recv()
        total = total + terms[step]
    for copy in copies:
        copy.wait_send()
    out[...] = total


def shards(panel, stiffness, mass, resident, face_rows, counts):
    n = lax.axis_size("row")
    columns = lax.axis_size("col")
    slots, nodes, width = panel.shape[1:]
    rows, kept = resident.shape[1:]
    face_n = face_rows.shape[2]
    quarter = face_n // columns
    own = kept // n
    bf16, f32 = jnp.bfloat16, jnp.float32
    dma = pltpu.SemaphoreType.DMA
    vmem = pl.BlockSpec(memory_space=pltpu.VMEM)
    smem = pl.BlockSpec(memory_space=pltpu.SMEM)
    anywhere = pl.BlockSpec(memory_space=pl.ANY)
    flops = 2 * slots * nodes * nodes * width + 2 * (rows + 2 * face_n) * kept * width
    return pl.pallas_call(
        functools.partial(gram_kernel, n),
        out_shape=jax.ShapeDtypeStruct((own, width), f32),
        in_specs=[anywhere, vmem, smem, smem, anywhere, anywhere],
        out_specs=vmem,
        scratch_shapes=[
            pltpu.VMEM((columns * slots, nodes, width), bf16),
            pltpu.VMEM((rows, kept), f32),
            pltpu.VMEM((rows, width), f32),
            pltpu.VMEM((DEPTH, nodes, nodes), bf16),
            pltpu.VMEM((slots, nodes, width), bf16),
            pltpu.VMEM((RES_DEPTH, nodes, kept), bf16),
            pltpu.VMEM((quarter // GROUP, GROUP, kept), f32),
            pltpu.VMEM((2 * PIECES, quarter, kept), bf16),
            pltpu.VMEM((PIECES, quarter, kept), bf16),
            pltpu.VMEM((quarter // GROUP, GROUP, width), f32),
            pltpu.VMEM((quarter // 2 // GROUP, GROUP, width), f32),
            pltpu.VMEM((2, quarter // 2, width), bf16),
            pltpu.VMEM((2, columns, quarter // 2, width), bf16),
            pltpu.VMEM((width, kept), f32),
            pltpu.VMEM((kept, width), f32),
            pltpu.VMEM((n - 1, own, width), f32),
            dma((DEPTH,)), dma((slots,)), dma((RES_DEPTH,)),
            dma((slots,)), dma((slots,)), dma((slots,)), dma((slots,)), dma((slots,)), dma((slots,)),
            dma((2,)), dma((2,)), dma((2,)), dma((2,)), dma((2,)), dma((2,)), dma((2,)), dma((2,)),
            dma((PIECES,)), dma((PIECES,)), dma((n - 1,)), dma((n - 1,)),
        ],
        compiler_params=pltpu.CompilerParams(
            collective_id=0, has_side_effects=True, vmem_limit_bytes=62 * 1024 * 1024),
        cost_estimate=pl.CostEstimate(
            flops=flops, bytes_accessed=2 * (slots * nodes * (nodes + width) + rows * kept), transcendentals=0),
    )(panel, mass.transpose(1, 0, 2), counts, face_rows, stiffness, resident)


def solution(mesh):
    in_specs = (
        P("row", "col", None, None),
        P("row", "col", None, None),
        P("row", "col", None),
        P("row", None, "col"),
        P("row", None, None),
        P("row"),
    )
    out_specs = P(("col", "row"), None)
    return jax.shard_map(shards, mesh=mesh, in_specs=in_specs, out_specs=out_specs, check_vma=False)
```

```python
import functools

import jax
import jax.numpy as jnp
from jax import lax
from jax.experimental import pallas as pl
from jax.experimental.pallas import tpu as pltpu
from jax.sharding import PartitionSpec as P

MESH = pl.DeviceIdType.MESH
ROWS_FIRST = (((0,), (0,)), ((), ()))
DEPTH = 4
RES_DEPTH = 16
PIECES = 4
GROUP = 8


def gram_kernel(
    n, panel, mass, counts, faces, stiffness, resident, out,
    applied, res, wide, kbuf, pbuf, rbuf, res_picked, res_rows, other_rows, picked, half_picked, near_rows, leaving, arrived, acc, gram, terms,
    k_sem, p_sem, r_sem, far_send, far_recv, mate_send, mate_recv, on_send, on_recv,
    face_send, face_recv, ffar_send, ffar_recv, fmate_send, fmate_recv, fon_send, fon_recv,
    row_send, row_recv, near_send, near_recv, sum_send, sum_recv,
):
    me = lax.axis_index("row")
    c = lax.axis_index("col")
    mate = (c // 2) * 2 + (1 - c % 2)
    far = (1 - c // 2) * 2 + c % 2
    opposite = (1 - c // 2) * 2 + (1 - c % 2)
    slots, nodes = panel.shape[1], panel.shape[2]
    face_n = faces.shape[2]
    quarter = face_n // PIECES
    half = quarter // 2
    following = jnp.minimum(me + 1, n - 1)
    own = out.shape[0]
    all_slots = applied.shape[0]

    def stiff_copy(e):
        return pltpu.make_async_copy(stiffness.at[0, e], kbuf.at[lax.rem(e, DEPTH)], k_sem.at[lax.rem(e, DEPTH)])

    def res_copy(s):
        rows = pl.ds(pl.multiple_of(s * nodes, nodes), nodes)
        return pltpu.make_async_copy(resident.at[0, rows], rbuf.at[lax.rem(s, RES_DEPTH)], r_sem.at[lax.rem(s, RES_DEPTH)])

    def panel_copy(e):
        return pltpu.make_async_copy(panel.at[0, e], pbuf.at[e], p_sem.at[e])

    def to(buffer, index, send, recv, k, column):
        return pltpu.make_async_remote_copy(
            src_ref=buffer.at[index], dst_ref=buffer.at[index], send_sem=send.at[k], recv_sem=recv.at[k],
            device_id=(column, me), device_id_type=MESH)

    for e in range(slots):
        if e < DEPTH:
            stiff_copy(jnp.int32(e)).start()
        panel_copy(e).start()
    for s in range(RES_DEPTH):
        res_copy(jnp.int32(s)).start()
    barrier = pltpu.get_barrier_semaphore()
    for step in range(1, n):
        pl.semaphore_signal(barrier, inc=1, device_id=(c, lax.rem(me + step, n)), device_id_type=MESH)
    for column in (mate, far):
        pl.semaphore_signal(barrier, inc=1, device_id=(column, me), device_id_type=MESH)
    pl.semaphore_wait(barrier, n + 1)

    acc[...] = jnp.zeros_like(acc)

    def node_weights(e):
        width = panel.shape[3]
        pieces = [jnp.broadcast_to(mass[e, :, k:k + width], (width, width)).T for k in range(0, nodes, width)]
        return jnp.concatenate(pieces, axis=0)

    def widen_resident(s):
        res_copy(s).wait()
        res[pl.ds(pl.multiple_of(s * nodes, nodes), nodes), :] = rbuf[lax.rem(s, RES_DEPTH)].astype(jnp.float32)

        @pl.when(s + RES_DEPTH < all_slots)
        def _():
            res_copy(s + RES_DEPTH).start()

    def apply_slot(e, carry):
        stiff_copy(e).wait()
        panel_copy(e).wait()
        values = pbuf[e]
        product = jnp.dot(kbuf[lax.rem(e, DEPTH)], values, preferred_element_type=jnp.float32)
        product = product + node_weights(e) * values.astype(jnp.float32)
        live = jnp.where(c * slots + e < counts[0], 1.0, 0.0)
        applied[c * slots + e] = (product * live).astype(jnp.bfloat16)
        to(applied, c * slots + e, far_send, far_recv, e, far).start()
        to(applied, c * slots + e, mate_send, mate_recv, e, mate).start()

        @pl.when(e + DEPTH < slots)
        def _():
            stiff_copy(e + DEPTH).start()

        for t in range(all_slots // slots):
            widen_resident(e * (all_slots // slots) + t)
        return carry

    lax.fori_loop(0, slots, apply_slot, 0)

    def add_slots(*which):
        total = None
        for slot in which:
            rows = pl.ds(pl.multiple_of(slot * nodes, nodes), nodes)
            block = applied[slot]
            wide[rows, :] = block.astype(jnp.float32)
            term = lax.dot_general(
                block, res[rows, :].astype(jnp.bfloat16), ROWS_FIRST, preferred_element_type=jnp.float32)
            total = term if total is None else total + term
        acc[...] += total

    def gather_rows(source, l, first, target, count, batch):
        def groups(i, carry):
            base = pl.multiple_of(first + i * batch, batch)
            rows = [faces[0, l, base + t] for t in range(batch)]
            values = [source[pl.ds(row, 1), :] for row in rows]
            for t, value in enumerate(values):
                target[i * (batch // GROUP) + t // GROUP, t % GROUP:t % GROUP + 1, :] = value
            return carry
        lax.fori_loop(0, count // batch, groups, 0)

    def row_copy(piece):
        return pltpu.make_async_remote_copy(
            src_ref=res_rows.at[piece], dst_ref=other_rows.at[piece],
            send_sem=row_send.at[piece], recv_sem=row_recv.at[piece],
            device_id=(c, following), device_id_type=MESH)

    def gather_resident(piece):
        gather_rows(res, 1 - lax.div(piece, PIECES), lax.rem(piece, PIECES) * quarter, res_picked, quarter, 32)
        res_rows[piece] = res_picked[...].reshape(quarter, res_picked.shape[2]).astype(jnp.bfloat16)

        @pl.when(jnp.logical_and(piece < PIECES, me < n - 1))
        def _():
            row_copy(piece).start()

    def near_slots(e):
        to(applied, mate * slots + e, mate_send, mate_recv, e, mate).wait_recv()
        add_slots(c * slots + e, mate * slots + e)

        @pl.when(e < 2 * PIECES)
        def _():
            gather_resident(e)

        to(applied, far * slots + e, far_send, far_recv, e, far).wait_recv()
        to(applied, far * slots + e, on_send, on_recv, e, mate).start()

    def exchange_slot(e, carry):
        near_slots(e)
        to(applied, opposite * slots + e - 1, on_send, on_recv, e - 1, mate).wait_recv()
        add_slots(far * slots + e, opposite * slots + e - 1)
        return carry

    near_slots(jnp.int32(0))
    add_slots(far * slots)
    lax.fori_loop(1, slots, exchange_slot, 0)
    to(applied, opposite * slots + slots - 1, on_send, on_recv, slots - 1, mate).wait_recv()
    add_slots(opposite * slots + slots - 1)

    def halves(h):
        return pl.ds(h * half, half)

    def face_copy(h):
        return pltpu.make_async_remote_copy(
            src_ref=leaving.at[h], dst_ref=arrived.at[c, halves(h)], send_sem=face_send.at[h],
            recv_sem=face_recv.at[h], device_id=(c, following), device_id_type=MESH)

    def share(h, column, send, recv, to_column):
        return to(arrived, (column, halves(h)), send, recv, h, to_column)

    def add_products(*pairs):
        total = None
        for left, right in pairs:
            term = lax.dot_general(left, right, ROWS_FIRST, preferred_element_type=jnp.float32)
            total = term if total is None else total + term
        acc[...] += total

    def face_pair(column):
        return arrived[column], res_rows[PIECES + column]

    def other_pair(piece):
        return near_rows[piece], other_rows[piece]

    mine, others = (c % 2) * (PIECES // 2), (1 - c % 2) * (PIECES // 2)

    def near_copy(k, first):
        return to(near_rows, first + k, near_send, near_recv, k, mate)

    def pick_near(k):
        gather_rows(wide, 0, (mine + k) * quarter, picked, quarter, 32)
        near_rows[mine + k] = picked[...].reshape(quarter, picked.shape[2]).astype(jnp.bfloat16)
        near_copy(k, mine).start()

    @pl.when(me < n - 1)
    def _():
        for h in range(2):
            gather_rows(wide, 1, c * quarter + h * half, half_picked, half, 32)
            leaving[h] = half_picked[...].reshape(half, half_picked.shape[2]).astype(jnp.bfloat16)
            face_copy(h).start()

    @pl.when(me > 0)
    def _():
        for h in range(2):
            pick_near(h)
            face_copy(h).wait_recv()
            share(h, c, ffar_send, ffar_recv, far).start()
            share(h, c, fmate_send, fmate_recv, mate).start()
        for piece in range(PIECES):
            row_copy(jnp.int32(piece)).wait_recv()
        add_products(other_pair(mine), other_pair(mine + 1))
        for h in range(2):
            share(h, far, ffar_send, ffar_recv, far).wait_recv()
            share(h, far, fon_send, fon_recv, mate).start()
            if h == 0:
                for k in range(2):
                    near_copy(k, others).wait_recv()
                add_products(other_pair(others), other_pair(others + 1))
        for h in range(2):
            share(h, mate, fmate_send, fmate_recv, mate).wait_recv()
        add_products(face_pair(c), face_pair(far), face_pair(mate))
        for h in range(2):
            share(h, opposite, fon_send, fon_recv, mate).wait_recv()
        add_products(face_pair(opposite))

    gram[...] = acc[...].T
    copies = []
    for step in range(1, n):
        peer = lax.rem(me + step, n)
        copy = pltpu.make_async_remote_copy(
            src_ref=gram.at[pl.ds(pl.multiple_of(peer * own, own), own)], dst_ref=terms.at[step - 1],
            send_sem=sum_send.at[step - 1], recv_sem=sum_recv.at[step - 1],
            device_id=(c, peer), device_id_type=MESH)
        copy.start()
        copies.append(copy)

    def drain(e, carry):
        to(applied, c * slots + e, far_send, far_recv, e, far).wait_send()
        to(applied, c * slots + e, mate_send, mate_recv, e, mate).wait_send()
        to(applied, far * slots + e, on_send, on_recv, e, mate).wait_send()
        return carry

    lax.fori_loop(0, slots, drain, 0)

    @pl.when(me < n - 1)
    def _():
        for h in range(2):
            face_copy(h).wait_send()
        for piece in range(PIECES):
            row_copy(jnp.int32(piece)).wait_send()

    @pl.when(me > 0)
    def _():
        for h in range(2):
            share(h, c, ffar_send, ffar_recv, far).wait_send()
            share(h, c, fmate_send, fmate_recv, mate).wait_send()
            share(h, far, fon_send, fon_recv, mate).wait_send()
            near_copy(h, mine).wait_send()

    total = gram[pl.ds(pl.multiple_of(me * own, own), own), :]
    for step, copy in enumerate(copies):
        copy.wait_recv()
        total = total + terms[step]
    for copy in copies:
        copy.wait_send()
    out[...] = total


def shards(panel, stiffness, mass, resident, face_rows, counts):
    n = lax.axis_size("row")
    columns = lax.axis_size("col")
    slots, nodes, width = panel.shape[1:]
    rows, kept = resident.shape[1:]
    face_n = face_rows.shape[2]
    quarter = face_n // columns
    own = kept // n
    bf16, f32 = jnp.bfloat16, jnp.float32
    dma = pltpu.SemaphoreType.DMA
    vmem = pl.BlockSpec(memory_space=pltpu.VMEM)
    smem = pl.BlockSpec(memory_space=pltpu.SMEM)
    anywhere = pl.BlockSpec(memory_space=pl.ANY)
    flops = 2 * slots * nodes * nodes * width + 2 * (rows + 2 * face_n) * kept * width
    return pl.pallas_call(
        functools.partial(gram_kernel, n),
        out_shape=jax.ShapeDtypeStruct((own, width), f32),
        in_specs=[anywhere, vmem, smem, smem, anywhere, anywhere],
        out_specs=vmem,
        scratch_shapes=[
            pltpu.VMEM((columns * slots, nodes, width), bf16),
            pltpu.VMEM((rows, kept), f32),
            pltpu.VMEM((rows, width), f32),
            pltpu.VMEM((DEPTH, nodes, nodes), bf16),
            pltpu.VMEM((slots, nodes, width), bf16),
            pltpu.VMEM((RES_DEPTH, nodes, kept), bf16),
            pltpu.VMEM((quarter // GROUP, GROUP, kept), f32),
            pltpu.VMEM((2 * PIECES, quarter, kept), bf16),
            pltpu.VMEM((PIECES, quarter, kept), bf16),
            pltpu.VMEM((quarter // GROUP, GROUP, width), f32),
            pltpu.VMEM((quarter // 2 // GROUP, GROUP, width), f32),
            pltpu.VMEM((PIECES, quarter, width), bf16),
            pltpu.VMEM((2, quarter // 2, width), bf16),
            pltpu.VMEM((columns, quarter, width), bf16),
            pltpu.VMEM((width, kept), f32),
            pltpu.VMEM((kept, width), f32),
            pltpu.VMEM((n - 1, own, width), f32),
            dma((DEPTH,)), dma((slots,)), dma((RES_DEPTH,)),
            dma((slots,)), dma((slots,)), dma((slots,)), dma((slots,)), dma((slots,)), dma((slots,)),
            dma((2,)), dma((2,)), dma((2,)), dma((2,)), dma((2,)), dma((2,)), dma((2,)), dma((2,)),
            dma((PIECES,)), dma((PIECES,)), dma((2,)), dma((2,)), dma((n - 1,)), dma((n - 1,)),
        ],
        compiler_params=pltpu.CompilerParams(
            collective_id=0, has_side_effects=True, vmem_limit_bytes=62 * 1024 * 1024),
        cost_estimate=pl.CostEstimate(
            flops=flops, bytes_accessed=2 * (slots * nodes * (nodes + width) + rows * kept), transcendentals=0),
    )(panel, mass.transpose(1, 0, 2), counts, face_rows, stiffness, resident)


def solution(mesh):
    in_specs = (
        P("row", "col", None, None),
        P("row", "col", None, None),
        P("row", "col", None),
        P("row", None, "col"),
        P("row", None, None),
        P("row"),
    )
    out_specs = P(("col", "row"), None)
    return jax.shard_map(shards, mesh=mesh, in_specs=in_specs, out_specs=out_specs, check_vma=False)
```

```python
import functools

import jax
import jax.numpy as jnp
from jax import lax
from jax.experimental import pallas as pl
from jax.experimental.pallas import tpu as pltpu
from jax.sharding import PartitionSpec as P

MESH = pl.DeviceIdType.MESH
ROWS_FIRST = (((0,), (0,)), ((), ()))
DEPTH = 4
RES_DEPTH = 16
PIECES = 4
AHEAD = 6
GROUP = 8


def gram_kernel(
    n, panel, mass, counts, faces, stiffness, resident, out,
    applied, res, wide, kbuf, pbuf, rbuf, res_picked, res_rows, other_rows, picked, half_picked, near_rows, leaving, arrived, acc, gram, terms,
    k_sem, p_sem, r_sem, far_send, far_recv, mate_send, mate_recv, on_send, on_recv,
    face_send, face_recv, ffar_send, ffar_recv, fmate_send, fmate_recv, fon_send, fon_recv,
    row_send, row_recv, near_send, near_recv, sum_send, sum_recv,
):
    me = lax.axis_index("row")
    c = lax.axis_index("col")
    mate = (c // 2) * 2 + (1 - c % 2)
    far = (1 - c // 2) * 2 + c % 2
    opposite = (1 - c // 2) * 2 + (1 - c % 2)
    slots, nodes = panel.shape[1], panel.shape[2]
    face_n = faces.shape[2]
    quarter = face_n // PIECES
    half = quarter // 2
    following = jnp.minimum(me + 1, n - 1)
    own = out.shape[0]
    all_slots = applied.shape[0]

    def stiff_copy(e):
        return pltpu.make_async_copy(stiffness.at[0, e], kbuf.at[lax.rem(e, DEPTH)], k_sem.at[lax.rem(e, DEPTH)])

    def res_copy(s):
        rows = pl.ds(pl.multiple_of(s * nodes, nodes), nodes)
        return pltpu.make_async_copy(resident.at[0, rows], rbuf.at[lax.rem(s, RES_DEPTH)], r_sem.at[lax.rem(s, RES_DEPTH)])

    def panel_copy(e):
        return pltpu.make_async_copy(panel.at[0, e], pbuf.at[e], p_sem.at[e])

    def to(buffer, index, send, recv, k, column):
        return pltpu.make_async_remote_copy(
            src_ref=buffer.at[index], dst_ref=buffer.at[index], send_sem=send.at[k], recv_sem=recv.at[k],
            device_id=(column, me), device_id_type=MESH)

    for e in range(slots):
        if e < DEPTH:
            stiff_copy(jnp.int32(e)).start()
        panel_copy(e).start()
    for s in range(RES_DEPTH):
        res_copy(jnp.int32(s)).start()
    barrier = pltpu.get_barrier_semaphore()
    for step in range(1, n):
        pl.semaphore_signal(barrier, inc=1, device_id=(c, lax.rem(me + step, n)), device_id_type=MESH)
    for column in (mate, far):
        pl.semaphore_signal(barrier, inc=1, device_id=(column, me), device_id_type=MESH)
    pl.semaphore_wait(barrier, n + 1)

    acc[...] = jnp.zeros_like(acc)

    def node_weights(e):
        width = panel.shape[3]
        pieces = [jnp.broadcast_to(mass[e, :, k:k + width], (width, width)).T for k in range(0, nodes, width)]
        return jnp.concatenate(pieces, axis=0)

    def widen_resident(s):
        res_copy(s).wait()
        res[pl.ds(pl.multiple_of(s * nodes, nodes), nodes), :] = rbuf[lax.rem(s, RES_DEPTH)].astype(jnp.float32)

        @pl.when(s + RES_DEPTH < all_slots)
        def _():
            res_copy(s + RES_DEPTH).start()

    def apply_slot(e, carry):
        stiff_copy(e).wait()
        panel_copy(e).wait()
        values = pbuf[e]
        product = jnp.dot(kbuf[lax.rem(e, DEPTH)], values, preferred_element_type=jnp.float32)
        product = product + node_weights(e) * values.astype(jnp.float32)
        live = jnp.where(c * slots + e < counts[0], 1.0, 0.0)
        applied[c * slots + e] = (product * live).astype(jnp.bfloat16)

        @pl.when(e < AHEAD)
        def _():
            to(applied, c * slots + e, far_send, far_recv, e, far).start()
        to(applied, c * slots + e, mate_send, mate_recv, e, mate).start()

        @pl.when(e + DEPTH < slots)
        def _():
            stiff_copy(e + DEPTH).start()

        for t in range(all_slots // slots):
            widen_resident(e * (all_slots // slots) + t)
        return carry

    lax.fori_loop(0, slots, apply_slot, 0)

    def add_slots(*which):
        total = None
        for slot in which:
            rows = pl.ds(pl.multiple_of(slot * nodes, nodes), nodes)
            block = applied[slot]
            wide[rows, :] = block.astype(jnp.float32)
            term = lax.dot_general(
                block, res[rows, :].astype(jnp.bfloat16), ROWS_FIRST, preferred_element_type=jnp.float32)
            total = term if total is None else total + term
        acc[...] += total

    def gather_rows(source, l, first, target, count, batch):
        def groups(i, carry):
            base = pl.multiple_of(first + i * batch, batch)
            rows = [faces[0, l, base + t] for t in range(batch)]
            values = [source[pl.ds(row, 1), :] for row in rows]
            for t, value in enumerate(values):
                target[i * (batch // GROUP) + t // GROUP, t % GROUP:t % GROUP + 1, :] = value
            return carry
        lax.fori_loop(0, count // batch, groups, 0)

    def row_copy(piece):
        return pltpu.make_async_remote_copy(
            src_ref=res_rows.at[piece], dst_ref=other_rows.at[piece],
            send_sem=row_send.at[piece], recv_sem=row_recv.at[piece],
            device_id=(c, following), device_id_type=MESH)

    def gather_resident(piece):
        gather_rows(res, 1 - lax.div(piece, PIECES), lax.rem(piece, PIECES) * quarter, res_picked, quarter, 32)
        res_rows[piece] = res_picked[...].reshape(quarter, res_picked.shape[2]).astype(jnp.bfloat16)

        @pl.when(jnp.logical_and(piece < PIECES, me < n - 1))
        def _():
            row_copy(piece).start()

    def near_slots(e):
        to(applied, mate * slots + e, mate_send, mate_recv, e, mate).wait_recv()
        add_slots(c * slots + e, mate * slots + e)

        @pl.when(e < 2 * PIECES)
        def _():
            gather_resident(e)

        to(applied, far * slots + e, far_send, far_recv, e, far).wait_recv()
        to(applied, far * slots + e, on_send, on_recv, e, mate).start()

        @pl.when(e + AHEAD < slots)
        def _():
            to(applied, c * slots + e + AHEAD, far_send, far_recv, e + AHEAD, far).start()

    def exchange_slot(e, carry):
        near_slots(e)
        to(applied, opposite * slots + e - 1, on_send, on_recv, e - 1, mate).wait_recv()
        add_slots(far * slots + e, opposite * slots + e - 1)
        return carry

    near_slots(jnp.int32(0))
    add_slots(far * slots)
    lax.fori_loop(1, slots, exchange_slot, 0)
    to(applied, opposite * slots + slots - 1, on_send, on_recv, slots - 1, mate).wait_recv()
    add_slots(opposite * slots + slots - 1)

    def halves(h):
        return pl.ds(h * half, half)

    def face_copy(h):
        return pltpu.make_async_remote_copy(
            src_ref=leaving.at[h], dst_ref=arrived.at[c, halves(h)], send_sem=face_send.at[h],
            recv_sem=face_recv.at[h], device_id=(c, following), device_id_type=MESH)

    def share(h, column, send, recv, to_column):
        return to(arrived, (column, halves(h)), send, recv, h, to_column)

    def add_products(*pairs):
        total = None
        for left, right in pairs:
            term = lax.dot_general(left, right, ROWS_FIRST, preferred_element_type=jnp.float32)
            total = term if total is None else total + term
        acc[...] += total

    def face_pair(column):
        return arrived[column], res_rows[PIECES + column]

    def other_pair(piece):
        return near_rows[piece], other_rows[piece]

    mine, others = (c % 2) * (PIECES // 2), (1 - c % 2) * (PIECES // 2)

    def near_copy(k, first):
        return to(near_rows, first + k, near_send, near_recv, k, mate)

    def pick_near(k):
        gather_rows(wide, 0, (mine + k) * quarter, picked, quarter, 32)
        near_rows[mine + k] = picked[...].reshape(quarter, picked.shape[2]).astype(jnp.bfloat16)
        near_copy(k, mine).start()

    @pl.when(me < n - 1)
    def _():
        for h in range(2):
            gather_rows(wide, 1, c * quarter + h * half, half_picked, half, 32)
            leaving[h] = half_picked[...].reshape(half, half_picked.shape[2]).astype(jnp.bfloat16)
            face_copy(h).start()

    @pl.when(me > 0)
    def _():
        for h in range(2):
            pick_near(h)
            face_copy(h).wait_recv()
            share(h, c, ffar_send, ffar_recv, far).start()
            share(h, c, fmate_send, fmate_recv, mate).start()
        for piece in range(PIECES):
            row_copy(jnp.int32(piece)).wait_recv()
        add_products(other_pair(mine), other_pair(mine + 1))
        for h in range(2):
            share(h, far, ffar_send, ffar_recv, far).wait_recv()
            share(h, far, fon_send, fon_recv, mate).start()
            if h == 0:
                for k in range(2):
                    near_copy(k, others).wait_recv()
                add_products(other_pair(others), other_pair(others + 1))
        for h in range(2):
            share(h, mate, fmate_send, fmate_recv, mate).wait_recv()
        add_products(face_pair(c), face_pair(far), face_pair(mate))
        for h in range(2):
            share(h, opposite, fon_send, fon_recv, mate).wait_recv()
        add_products(face_pair(opposite))

    gram[...] = acc[...].T
    copies = []
    for step in range(1, n):
        peer = lax.rem(me + step, n)
        copy = pltpu.make_async_remote_copy(
            src_ref=gram.at[pl.ds(pl.multiple_of(peer * own, own), own)], dst_ref=terms.at[step - 1],
            send_sem=sum_send.at[step - 1], recv_sem=sum_recv.at[step - 1],
            device_id=(c, peer), device_id_type=MESH)
        copy.start()
        copies.append(copy)

    def drain(e, carry):
        to(applied, c * slots + e, far_send, far_recv, e, far).wait_send()
        to(applied, c * slots + e, mate_send, mate_recv, e, mate).wait_send()
        to(applied, far * slots + e, on_send, on_recv, e, mate).wait_send()
        return carry

    lax.fori_loop(0, slots, drain, 0)

    @pl.when(me < n - 1)
    def _():
        for h in range(2):
            face_copy(h).wait_send()
        for piece in range(PIECES):
            row_copy(jnp.int32(piece)).wait_send()

    @pl.when(me > 0)
    def _():
        for h in range(2):
            share(h, c, ffar_send, ffar_recv, far).wait_send()
            share(h, c, fmate_send, fmate_recv, mate).wait_send()
            share(h, far, fon_send, fon_recv, mate).wait_send()
            near_copy(h, mine).wait_send()

    total = gram[pl.ds(pl.multiple_of(me * own, own), own), :]
    for step, copy in enumerate(copies):
        copy.wait_recv()
        total = total + terms[step]
    for copy in copies:
        copy.wait_send()
    out[...] = total


def shards(panel, stiffness, mass, resident, face_rows, counts):
    n = lax.axis_size("row")
    columns = lax.axis_size("col")
    slots, nodes, width = panel.shape[1:]
    rows, kept = resident.shape[1:]
    face_n = face_rows.shape[2]
    quarter = face_n // columns
    own = kept // n
    bf16, f32 = jnp.bfloat16, jnp.float32
    dma = pltpu.SemaphoreType.DMA
    vmem = pl.BlockSpec(memory_space=pltpu.VMEM)
    smem = pl.BlockSpec(memory_space=pltpu.SMEM)
    anywhere = pl.BlockSpec(memory_space=pl.ANY)
    flops = 2 * slots * nodes * nodes * width + 2 * (rows + 2 * face_n) * kept * width
    return pl.pallas_call(
        functools.partial(gram_kernel, n),
        out_shape=jax.ShapeDtypeStruct((own, width), f32),
        in_specs=[anywhere, vmem, smem, smem, anywhere, anywhere],
        out_specs=vmem,
        scratch_shapes=[
            pltpu.VMEM((columns * slots, nodes, width), bf16),
            pltpu.VMEM((rows, kept), f32),
            pltpu.VMEM((rows, width), f32),
            pltpu.VMEM((DEPTH, nodes, nodes), bf16),
            pltpu.VMEM((slots, nodes, width), bf16),
            pltpu.VMEM((RES_DEPTH, nodes, kept), bf16),
            pltpu.VMEM((quarter // GROUP, GROUP, kept), f32),
            pltpu.VMEM((2 * PIECES, quarter, kept), bf16),
            pltpu.VMEM((PIECES, quarter, kept), bf16),
            pltpu.VMEM((quarter // GROUP, GROUP, width), f32),
            pltpu.VMEM((quarter // 2 // GROUP, GROUP, width), f32),
            pltpu.VMEM((PIECES, quarter, width), bf16),
            pltpu.VMEM((2, quarter // 2, width), bf16),
            pltpu.VMEM((columns, quarter, width), bf16),
            pltpu.VMEM((width, kept), f32),
            pltpu.VMEM((kept, width), f32),
            pltpu.VMEM((n - 1, own, width), f32),
            dma((DEPTH,)), dma((slots,)), dma((RES_DEPTH,)),
            dma((slots,)), dma((slots,)), dma((slots,)), dma((slots,)), dma((slots,)), dma((slots,)),
            dma((2,)), dma((2,)), dma((2,)), dma((2,)), dma((2,)), dma((2,)), dma((2,)), dma((2,)),
            dma((PIECES,)), dma((PIECES,)), dma((2,)), dma((2,)), dma((n - 1,)), dma((n - 1,)),
        ],
        compiler_params=pltpu.CompilerParams(
            collective_id=0, has_side_effects=True, vmem_limit_bytes=62 * 1024 * 1024),
        cost_estimate=pl.CostEstimate(
            flops=flops, bytes_accessed=2 * (slots * nodes * (nodes + width) + rows * kept), transcendentals=0),
    )(panel, mass.transpose(1, 0, 2), counts, face_rows, stiffness, resident)


def solution(mesh):
    in_specs = (
        P("row", "col", None, None),
        P("row", "col", None, None),
        P("row", "col", None),
        P("row", None, "col"),
        P("row", None, None),
        P("row"),
    )
    out_specs = P(("col", "row"), None)
    return jax.shard_map(shards, mesh=mesh, in_specs=in_specs, out_specs=out_specs, check_vma=False)
```

```python
import functools

import jax
import jax.numpy as jnp
from jax import lax
from jax.experimental import pallas as pl
from jax.experimental.pallas import tpu as pltpu
from jax.sharding import PartitionSpec as P

MESH = pl.DeviceIdType.MESH
ROWS_FIRST = (((0,), (0,)), ((), ()))
DEPTH = 4
RES_DEPTH = 16
PIECES = 4
AHEAD = 6
GROUP = 8


def gram_kernel(
    n, panel, mass, counts, faces, stiffness, resident, out,
    applied, res, wide, kbuf, pbuf, rbuf, res_picked, res_rows, other_rows, picked, half_picked, near_rows, leaving, arrived, acc, gram, terms,
    k_sem, p_sem, r_sem, far_send, far_recv, mate_send, mate_recv, on_send, on_recv,
    face_send, face_recv, ffar_send, ffar_recv, fmate_send, fmate_recv, fon_send, fon_recv,
    row_send, row_recv, near_send, near_recv, sum_send, sum_recv,
):
    me = lax.axis_index("row")
    c = lax.axis_index("col")
    mate = (c // 2) * 2 + (1 - c % 2)
    far = (1 - c // 2) * 2 + c % 2
    opposite = (1 - c // 2) * 2 + (1 - c % 2)
    slots, nodes = panel.shape[1], panel.shape[2]
    face_n = faces.shape[2]
    quarter = face_n // PIECES
    half = quarter // 2
    following = jnp.minimum(me + 1, n - 1)
    own = out.shape[0]
    all_slots = applied.shape[0]

    def stiff_copy(e):
        return pltpu.make_async_copy(stiffness.at[0, e], kbuf.at[lax.rem(e, DEPTH)], k_sem.at[lax.rem(e, DEPTH)])

    def res_copy(s):
        rows = pl.ds(pl.multiple_of(s * nodes, nodes), nodes)
        return pltpu.make_async_copy(resident.at[0, rows], rbuf.at[lax.rem(s, RES_DEPTH)], r_sem.at[lax.rem(s, RES_DEPTH)])

    def panel_copy(e):
        return pltpu.make_async_copy(panel.at[0, e], pbuf.at[e], p_sem.at[e])

    def to(buffer, index, send, recv, k, column):
        return pltpu.make_async_remote_copy(
            src_ref=buffer.at[index], dst_ref=buffer.at[index], send_sem=send.at[k], recv_sem=recv.at[k],
            device_id=(column, me), device_id_type=MESH)

    for e in range(slots):
        if e < DEPTH:
            stiff_copy(jnp.int32(e)).start()
        panel_copy(e).start()
    for s in range(RES_DEPTH):
        res_copy(jnp.int32(s)).start()
    barrier = pltpu.get_barrier_semaphore()
    for step in range(1, n):
        pl.semaphore_signal(barrier, inc=1, device_id=(c, lax.rem(me + step, n)), device_id_type=MESH)
    for column in (mate, far):
        pl.semaphore_signal(barrier, inc=1, device_id=(column, me), device_id_type=MESH)
    pl.semaphore_wait(barrier, n + 1)

    acc[...] = jnp.zeros_like(acc)

    def node_weights(e):
        width = panel.shape[3]
        pieces = [jnp.broadcast_to(mass[e, :, k:k + width], (width, width)).T for k in range(0, nodes, width)]
        return jnp.concatenate(pieces, axis=0)

    def widen_resident(s):
        res_copy(s).wait()
        res[pl.ds(pl.multiple_of(s * nodes, nodes), nodes), :] = rbuf[lax.rem(s, RES_DEPTH)].astype(jnp.float32)

        @pl.when(s + RES_DEPTH < all_slots)
        def _():
            res_copy(s + RES_DEPTH).start()

    def apply_slot(e, carry):
        stiff_copy(e).wait()
        panel_copy(e).wait()
        values = pbuf[e]
        product = jnp.dot(kbuf[lax.rem(e, DEPTH)], values, preferred_element_type=jnp.float32)
        product = product + node_weights(e) * values.astype(jnp.float32)
        live = jnp.where(c * slots + e < counts[0], 1.0, 0.0)
        applied[c * slots + e] = (product * live).astype(jnp.bfloat16)

        @pl.when(e < AHEAD)
        def _():
            to(applied, c * slots + e, far_send, far_recv, e, far).start()
        to(applied, c * slots + e, mate_send, mate_recv, e, mate).start()

        @pl.when(e + DEPTH < slots)
        def _():
            stiff_copy(e + DEPTH).start()

        for t in range(all_slots // slots):
            widen_resident(e * (all_slots // slots) + t)
        return carry

    lax.fori_loop(0, slots, apply_slot, 0)

    def add_slots(*which):
        total = None
        for slot in which:
            rows = pl.ds(pl.multiple_of(slot * nodes, nodes), nodes)
            block = applied[slot]
            wide[rows, :] = block.astype(jnp.float32)
            term = lax.dot_general(
                block, res[rows, :].astype(jnp.bfloat16), ROWS_FIRST, preferred_element_type=jnp.float32)
            total = term if total is None else total + term
        acc[...] += total

    def gather_rows(source, l, first, target, count, batch):
        def groups(i, carry):
            base = pl.multiple_of(first + i * batch, batch)
            rows = [faces[0, l, base + t] for t in range(batch)]
            values = [source[pl.ds(row, 1), :] for row in rows]
            for t, value in enumerate(values):
                target[i * (batch // GROUP) + t // GROUP, t % GROUP:t % GROUP + 1, :] = value
            return carry
        lax.fori_loop(0, count // batch, groups, 0)

    def row_copy(piece):
        return pltpu.make_async_remote_copy(
            src_ref=res_rows.at[piece], dst_ref=other_rows.at[piece],
            send_sem=row_send.at[piece], recv_sem=row_recv.at[piece],
            device_id=(c, following), device_id_type=MESH)

    def gather_resident(piece):
        gather_rows(res, 1 - lax.div(piece, PIECES), lax.rem(piece, PIECES) * quarter, res_picked, quarter, 32)
        res_rows[piece] = res_picked[...].reshape(quarter, res_picked.shape[2]).astype(jnp.bfloat16)

        @pl.when(jnp.logical_and(piece < PIECES, me < n - 1))
        def _():
            row_copy(piece).start()

    def far_slot(e):
        to(applied, far * slots + e, far_send, far_recv, e, far).wait_recv()
        to(applied, far * slots + e, on_send, on_recv, e, mate).start()

        @pl.when(e + AHEAD < slots)
        def _():
            to(applied, c * slots + e + AHEAD, far_send, far_recv, e + AHEAD, far).start()

        @pl.when(e < 2 * PIECES)
        def _():
            gather_resident(e)

        to(applied, mate * slots + e, mate_send, mate_recv, e, mate).wait_recv()

    def exchange_slot(e, carry):
        far_slot(e)
        to(applied, opposite * slots + e - 1, on_send, on_recv, e - 1, mate).wait_recv()
        add_slots(c * slots + e, mate * slots + e, far * slots + e, opposite * slots + e - 1)
        return carry

    far_slot(jnp.int32(0))
    add_slots(c * slots, mate * slots, far * slots)
    lax.fori_loop(1, slots, exchange_slot, 0)
    to(applied, opposite * slots + slots - 1, on_send, on_recv, slots - 1, mate).wait_recv()
    add_slots(opposite * slots + slots - 1)

    def halves(h):
        return pl.ds(h * half, half)

    def face_copy(h):
        return pltpu.make_async_remote_copy(
            src_ref=leaving.at[h], dst_ref=arrived.at[c, halves(h)], send_sem=face_send.at[h],
            recv_sem=face_recv.at[h], device_id=(c, following), device_id_type=MESH)

    def share(h, column, send, recv, to_column):
        return to(arrived, (column, halves(h)), send, recv, h, to_column)

    def add_products(*pairs):
        total = None
        for left, right in pairs:
            term = lax.dot_general(left, right, ROWS_FIRST, preferred_element_type=jnp.float32)
            total = term if total is None else total + term
        acc[...] += total

    def face_pair(column):
        return arrived[column], res_rows[PIECES + column]

    def other_pair(piece):
        return near_rows[piece], other_rows[piece]

    mine, others = (c % 2) * (PIECES // 2), (1 - c % 2) * (PIECES // 2)

    def near_copy(k, first):
        return to(near_rows, first + k, near_send, near_recv, k, mate)

    def pick_near(k):
        gather_rows(wide, 0, (mine + k) * quarter, picked, quarter, 32)
        near_rows[mine + k] = picked[...].reshape(quarter, picked.shape[2]).astype(jnp.bfloat16)
        near_copy(k, mine).start()

    @pl.when(me < n - 1)
    def _():
        for h in range(2):
            gather_rows(wide, 1, c * quarter + h * half, half_picked, half, 32)
            leaving[h] = half_picked[...].reshape(half, half_picked.shape[2]).astype(jnp.bfloat16)
            face_copy(h).start()

    @pl.when(me > 0)
    def _():
        for h in range(2):
            pick_near(h)
            face_copy(h).wait_recv()
            share(h, c, ffar_send, ffar_recv, far).start()
            share(h, c, fmate_send, fmate_recv, mate).start()
        for piece in range(PIECES):
            row_copy(jnp.int32(piece)).wait_recv()
        add_products(other_pair(mine), other_pair(mine + 1))
        for h in range(2):
            share(h, far, ffar_send, ffar_recv, far).wait_recv()
            share(h, far, fon_send, fon_recv, mate).start()
            if h == 0:
                for k in range(2):
                    near_copy(k, others).wait_recv()
                add_products(other_pair(others), other_pair(others + 1))
        for h in range(2):
            share(h, mate, fmate_send, fmate_recv, mate).wait_recv()
        add_products(face_pair(c), face_pair(far), face_pair(mate))
        for h in range(2):
            share(h, opposite, fon_send, fon_recv, mate).wait_recv()
        add_products(face_pair(opposite))

    gram[...] = acc[...].T
    copies = []
    for step in range(1, n):
        peer = lax.rem(me + step, n)
        copy = pltpu.make_async_remote_copy(
            src_ref=gram.at[pl.ds(pl.multiple_of(peer * own, own), own)], dst_ref=terms.at[step - 1],
            send_sem=sum_send.at[step - 1], recv_sem=sum_recv.at[step - 1],
            device_id=(c, peer), device_id_type=MESH)
        copy.start()
        copies.append(copy)

    def drain(e, carry):
        to(applied, c * slots + e, far_send, far_recv, e, far).wait_send()
        to(applied, c * slots + e, mate_send, mate_recv, e, mate).wait_send()
        to(applied, far * slots + e, on_send, on_recv, e, mate).wait_send()
        return carry

    lax.fori_loop(0, slots, drain, 0)

    @pl.when(me < n - 1)
    def _():
        for h in range(2):
            face_copy(h).wait_send()
        for piece in range(PIECES):
            row_copy(jnp.int32(piece)).wait_send()

    @pl.when(me > 0)
    def _():
        for h in range(2):
            share(h, c, ffar_send, ffar_recv, far).wait_send()
            share(h, c, fmate_send, fmate_recv, mate).wait_send()
            share(h, far, fon_send, fon_recv, mate).wait_send()
            near_copy(h, mine).wait_send()

    total = gram[pl.ds(pl.multiple_of(me * own, own), own), :]
    for step, copy in enumerate(copies):
        copy.wait_recv()
        total = total + terms[step]
    for copy in copies:
        copy.wait_send()
    out[...] = total


def shards(panel, stiffness, mass, resident, face_rows, counts):
    n = lax.axis_size("row")
    columns = lax.axis_size("col")
    slots, nodes, width = panel.shape[1:]
    rows, kept = resident.shape[1:]
    face_n = face_rows.shape[2]
    quarter = face_n // columns
    own = kept // n
    bf16, f32 = jnp.bfloat16, jnp.float32
    dma = pltpu.SemaphoreType.DMA
    vmem = pl.BlockSpec(memory_space=pltpu.VMEM)
    smem = pl.BlockSpec(memory_space=pltpu.SMEM)
    anywhere = pl.BlockSpec(memory_space=pl.ANY)
    flops = 2 * slots * nodes * nodes * width + 2 * (rows + 2 * face_n) * kept * width
    return pl.pallas_call(
        functools.partial(gram_kernel, n),
        out_shape=jax.ShapeDtypeStruct((own, width), f32),
        in_specs=[anywhere, vmem, smem, smem, anywhere, anywhere],
        out_specs=vmem,
        scratch_shapes=[
            pltpu.VMEM((columns * slots, nodes, width), bf16),
            pltpu.VMEM((rows, kept), f32),
            pltpu.VMEM((rows, width), f32),
            pltpu.VMEM((DEPTH, nodes, nodes), bf16),
            pltpu.VMEM((slots, nodes, width), bf16),
            pltpu.VMEM((RES_DEPTH, nodes, kept), bf16),
            pltpu.VMEM((quarter // GROUP, GROUP, kept), f32),
            pltpu.VMEM((2 * PIECES, quarter, kept), bf16),
            pltpu.VMEM((PIECES, quarter, kept), bf16),
            pltpu.VMEM((quarter // GROUP, GROUP, width), f32),
            pltpu.VMEM((quarter // 2 // GROUP, GROUP, width), f32),
            pltpu.VMEM((PIECES, quarter, width), bf16),
            pltpu.VMEM((2, quarter // 2, width), bf16),
            pltpu.VMEM((columns, quarter, width), bf16),
            pltpu.VMEM((width, kept), f32),
            pltpu.VMEM((kept, width), f32),
            pltpu.VMEM((n - 1, own, width), f32),
            dma((DEPTH,)), dma((slots,)), dma((RES_DEPTH,)),
            dma((slots,)), dma((slots,)), dma((slots,)), dma((slots,)), dma((slots,)), dma((slots,)),
            dma((2,)), dma((2,)), dma((2,)), dma((2,)), dma((2,)), dma((2,)), dma((2,)), dma((2,)),
            dma((PIECES,)), dma((PIECES,)), dma((2,)), dma((2,)), dma((n - 1,)), dma((n - 1,)),
        ],
        compiler_params=pltpu.CompilerParams(
            collective_id=0, has_side_effects=True, vmem_limit_bytes=62 * 1024 * 1024),
        cost_estimate=pl.CostEstimate(
            flops=flops, bytes_accessed=2 * (slots * nodes * (nodes + width) + rows * kept), transcendentals=0),
    )(panel, mass.transpose(1, 0, 2), counts, face_rows, stiffness, resident)


def solution(mesh):
    in_specs = (
        P("row", "col", None, None),
        P("row", "col", None, None),
        P("row", "col", None),
        P("row", None, "col"),
        P("row", None, None),
        P("row"),
    )
    out_specs = P(("col", "row"), None)
    return jax.shard_map(shards, mesh=mesh, in_specs=in_specs, out_specs=out_specs, check_vma=False)
```
